32 devices in a mesh: row: 4 (over z), wide: 8 (over y, x, core).
Axes of the slice: x: 2, y: 2, z: 4, core: 2. Of those that a mesh axis runs over, the one named last changes fastest.
Arguments:
- hidden: bfloat16 [4096, 2048], P(('row', 'wide')), may hold values from -6 to 6
- modality: int32 [4096], P(('row', 'wide')), may hold values from 0 to 2
- norm_gain: bfloat16 [2048], replicated, may hold values from 0.099609375 to 1.8984375
- in_proj: bfloat16 [3, 2048, 2, 4096], P(None, None, None, 'wide'), may hold values from -0.125 to 0.125
- conv_weight: bfloat16 [4, 4096], P(None, 'wide'), may hold values from -3 to 3
- conv_bias: bfloat16 [4096], P('wide'), may hold values from -3 to 3
- x_proj_dt: bfloat16 [4096, 128], replicated, may hold values from -0.09375 to 0.09375
- x_proj_bc: bfloat16 [4096, 32], replicated, may hold values from -0.09375 to 0.09375
- dt_proj: bfloat16 [128, 4096], replicated, may hold values from -0.5 to 0.5
- dt_bias: float32 [4096], replicated, may hold values from -5 to -3
- a_log: float32 [16, 4096], replicated, may hold values from -8 to 0.2
- skip_weight: float32 [4096], replicated, may hold values from 0.5 to 1.5
- out_proj: bfloat16 [3, 4096, 2048], P(None, 'wide'), may hold values from -0.09375 to 0.09375
- cotangent: bfloat16 [4096, 2048], P(('row', 'wide')), may hold values from -6 to 6
Outputs:
- output: bfloat16 [4096, 2048], P(('row', 'wide'))
- grad_hidden: float32 [4096, 2048], P(('row', 'wide'))
- grad_norm_gain: float32 [2048], P('wide')
- grad_in_proj: float32 [3, 2048, 2, 4096], P(None, None, None, 'wide')
- grad_conv_weight: float32 [4, 4096], P(None, 'wide')
- grad_conv_bias: float32 [4096], P('wide')
- grad_x_proj_dt: float32 [4096, 128], P('wide')
- grad_x_proj_bc: float32 [4096, 32], P('wide')
- grad_dt_proj: float32 [128, 4096], P(None, 'wide')
- grad_dt_bias: float32 [4096], P('wide')
- grad_a_log: float32 [16, 4096], P(None, 'wide')
- grad_skip_weight: float32 [4096], P('wide')
- grad_out_proj: float32 [3, 4096, 2048], P(None, 'wide')
The draws below stay inside these ranges and needn't reach their ends.
All inputs are finite; a program needn't handle non-finite values.
Results may differ from the reference program's by a relative error of at most 0.02.
Values may be sent and summed in bfloat16 or wider, within the bound.
No kernel may reach another device: no remote copies, remote signals or barrier semaphores. Data moves between devices by JAX's collectives and lax.ppermute only.
A program may use at most 320 MiB of HBM per device.

```python
import jax
import jax.numpy as jnp
from jax import lax

D = 2048
INNER = 4096
N_STATE = 16
DT_RANK = 128
CONV = 4
MODS = 3
SEQ_LEN = 1024
TOKENS = 4096
N_ROW = 4


def with_ends(drawn, rng, smallest, largest):
    dims = drawn.shape
    index_at = [jax.random.randint(jax.random.fold_in(rng, axis), (), 0, dims[axis]) for axis in range(len(dims))]
    drawn = drawn.at[tuple(index_at)].set(smallest)
    longest = dims.index(max(dims))
    index_at[longest] = (index_at[longest] + 1) % dims[longest]
    return drawn.at[tuple(index_at)].set(largest)


def levels(own_key, dims, cuts, least, top_value):
    gain, own = 1.0, jax.random.fold_in(own_key, 6)
    for dim, parts in cuts:
        steps = jnp.exp(jax.random.uniform(jax.random.fold_in(own, dim), (parts,), jnp.float32, least / len(cuts), top_value / len(cuts)))
        gain = gain * jnp.repeat(steps, dims[dim] // parts).reshape([-1 if axis == dim else 1 for axis in range(len(dims))])
    return gain


def gaussian(rng, extent, width, most, split=(), held_as=jnp.bfloat16):
    values = jax.random.normal(rng, extent, jnp.float32) * width
    if len(split) > 0:
        values = levels(rng, extent, split, -0.22, 0.18) * values
    return jnp.clip(values, min=-most, max=most).astype(held_as)


def setup_inputs(seed: int = 0) -> dict:
    streams_of = jax.random.split(jax.random.key(seed), 15)
    return {
        "hidden": gaussian(streams_of[0], (TOKENS, D), 1.0, 6.0, ((0, 32),)),
        "modality": with_ends(jax.random.randint(streams_of[1], (TOKENS,), 0, MODS), jax.random.fold_in(streams_of[1], 1), 0, MODS - 1).astype(jnp.int32),
        "norm_gain": jnp.clip(1.0 + 0.18 * jax.random.normal(streams_of[2], (D,), jnp.float32), 0.099609375, 1.8984375).astype(jnp.bfloat16),
        "in_proj": gaussian(streams_of[3], (MODS, D, 2, INNER), D ** -0.5, 0.125, ((3, 8),)),
        "conv_weight": gaussian(streams_of[4], (CONV, INNER), CONV ** -0.5, 3.0, ((1, 8),)),
        "conv_bias": gaussian(streams_of[5], (INNER,), 0.5, 3.0, ((0, 8),)),
        "x_proj_dt": gaussian(streams_of[6], (INNER, DT_RANK), INNER ** -0.5, 0.09375),
        "x_proj_bc": gaussian(streams_of[7], (INNER, 2 * N_STATE), INNER ** -0.5, 0.09375),
        "dt_proj": gaussian(streams_of[8], (DT_RANK, INNER), DT_RANK ** -0.5, 0.5),
        "dt_bias": jnp.clip(jax.random.uniform(streams_of[9], (INNER,), jnp.float32, -5.0, -3.0), -5.0, -3.0),
        "a_log": jnp.clip(jax.random.uniform(streams_of[10], (N_STATE, INNER), jnp.float32, -8.0, 0.2), -8.0, 0.2),
        "skip_weight": jnp.clip(jax.random.uniform(streams_of[11], (INNER,), jnp.float32, 0.5, 1.5), 0.5, 1.5),
        "out_proj": gaussian(streams_of[12], (MODS, INNER, D), INNER ** -0.5, 0.09375, ((1, 8),)),
        "cotangent": gaussian(streams_of[13], (TOKENS, D), 1.0, 6.0, ((0, 32),)),
    }


EPS = 1e-05
HIGHEST = lax.Precision.HIGHEST

@jax.custom_vjp
def low(v):
    return lax.optimization_barrier(v.astype(jnp.bfloat16)).astype(jnp.float32)

@jax.custom_vjp
def low_back(v):
    return v

def low_keep(v):
    return (low(v), None)

def low_pass(kept, grad):
    return (grad,)

def back_keep(v):
    return (v, None)

def back_low(kept, grad):
    return (low(grad),)
low.defvjp(low_keep, low_pass)
low_back.defvjp(back_keep, back_low)

def combine(earlier_pair, later_pair):
    decay_one, state_one = earlier_pair
    decay_two, state_two = later_pair
    return (decay_one * decay_two, decay_two * state_one + state_two)

def product(left, right):
    return jnp.dot(left, right, precision=HIGHEST)

def modal_product(rows, modal_ids, weights):
    order = jnp.argsort(modal_ids, stable=True).astype(jnp.int32)
    inverse = jnp.argsort(order).astype(jnp.int32)
    sorted_rows = rows[order]
    sorted_ids = modal_ids[order]
    row_count = rows.shape[0]
    span_rows = min(256, row_count)
    while row_count % span_rows:
        span_rows = span_rows // 2
    block_count = row_count // span_rows
    out_cols = weights.shape[2]

    def block_product(pieces):
        block, id_block = pieces
        running = jnp.zeros((span_rows, out_cols), block.dtype)
        for modal_id in range(MODS):

            def take_block():
                return jnp.where((id_block == modal_id)[:, None], product(block, weights[modal_id]), jnp.zeros((span_rows, out_cols), block.dtype))

            def skip_block():
                return jnp.zeros((span_rows, out_cols), block.dtype)
            present = (id_block[0] <= modal_id) & (modal_id <= id_block[-1])
            running = running + lax.cond(present, take_block, skip_block)
        return running
    result = lax.map(block_product, (sorted_rows.reshape(block_count, span_rows, rows.shape[1]), sorted_ids.reshape(block_count, span_rows)))
    return result.reshape(row_count, out_cols)[inverse]

def selective(steps_dt, values, coefs, decay_rate, skip_gain):
    block_size = min(64, SEQ_LEN)
    block_count = SEQ_LEN // block_size

    def to_blocks(tensor):
        return jnp.moveaxis(tensor.reshape(N_ROW, block_count, block_size, tensor.shape[-1]), 1, 0)

    @jax.checkpoint
    def advance(carried, pieces):
        step_block, value_block, coef_block = pieces
        input_coef = coef_block[..., :N_STATE]
        output_coef = coef_block[..., N_STATE:]
        factor = jnp.exp(step_block[:, :, None, :] * decay_rate)
        inject = (step_block * value_block)[:, :, None, :] * input_coef[..., None]
        decay_run, local_part = lax.associative_scan(combine, (factor, inject), axis=1)
        states = local_part + decay_run * carried[:, None]
        result = lax.optimization_barrier(jnp.sum(states * output_coef[..., None], axis=2)) + skip_gain * value_block
        return (states[:, -1], result)
    initial = jnp.zeros((N_ROW, N_STATE, INNER), jnp.float32)
    _, outputs = lax.scan(advance, initial, (to_blocks(steps_dt), to_blocks(values), to_blocks(coefs)))
    return jnp.moveaxis(outputs, 0, 1).reshape(TOKENS, INNER)

def reference(hidden, modality, norm_gain, in_proj, conv_weight, conv_bias, x_proj_dt, x_proj_bc, dt_proj, dt_bias, a_log, skip_weight, out_proj, cotangent):
    modal_ids = modality.astype(jnp.int32)

    def layer(residual, gain_vec, in_weight, conv_taps, conv_shift, proj_dt, proj_bc, dt_weight, dt_shift, log_decay, skip_gain, out_weight):
        inv_rms = lax.rsqrt(lax.optimization_barrier(jnp.mean(residual * residual, axis=-1, keepdims=True)) + EPS)
        normed = low(residual * inv_rms * gain_vec)
        mixed_proj = modal_product(normed, modal_ids, in_weight.reshape(MODS, D, 2 * INNER))
        mixed_proj = low_back(mixed_proj)
        conv_in = mixed_proj[:, :INNER].reshape(N_ROW, SEQ_LEN, INNER)
        gate_in = mixed_proj[:, INNER:]
        padded = jnp.pad(conv_in, ((0, 0), (CONV - 1, 0), (0, 0)))
        pre_act = conv_shift + conv_taps[0] * padded[:, 0:SEQ_LEN]
        for offset in range(1, CONV):
            pre_act = pre_act + conv_taps[offset] * padded[:, offset:offset + SEQ_LEN]
        conv_out = low_back(low(jax.nn.silu(pre_act))).reshape(TOKENS, INNER)
        low_rank = low_back(low(product(conv_out, proj_dt)))
        coefs = low_back(product(conv_out, proj_bc))
        steps_dt = jax.nn.softplus(low_back(product(low_rank, dt_weight) + dt_shift))
        scanned = selective(steps_dt, conv_out, coefs, -jnp.exp(log_decay), skip_gain)
        gate_y = low_back(low(scanned))
        gated = low(gate_y * jax.nn.silu(gate_in))
        projected = modal_product(gated, modal_ids, out_weight)
        return residual + projected
    primal = tuple((argument.astype(jnp.float32) for argument in (hidden, norm_gain, in_proj, conv_weight, conv_bias, x_proj_dt, x_proj_bc, dt_proj, dt_bias, a_log, skip_weight, out_proj)))
    output, pullback = jax.vjp(layer, *primal)
    gradients = pullback(cotangent.astype(jnp.float32))
    return (output.astype(jnp.bfloat16), gradients[0], gradients[1], gradients[2], gradients[3], gradients[4], gradients[5], gradients[6], gradients[7], gradients[8], gradients[9], gradients[10], gradients[11])
```

```python
import functools

import jax
import jax.numpy as jnp
from jax import lax
from jax.experimental import pallas as pl
from jax.experimental.pallas import tpu as pltpu
from jax.sharding import PartitionSpec as P
LOG2E = 1.4426950408889634
EPS = 1e-05
SPAN = 256
TILE = 16
FU, BU = 4, 2

def softplus(v):
    return jnp.maximum(v, 0.0) + jnp.log1p(jnp.exp(-jnp.abs(v)))

def spread(columns, n):
    wide = TILE * n
    pick = lax.broadcasted_iota(jnp.int32, (n, wide), 1) % n == lax.broadcasted_iota(jnp.int32, (n, wide), 0)
    tiled = jnp.dot(columns.astype(jnp.bfloat16), pick.astype(jnp.bfloat16), preferred_element_type=jnp.float32)
    return jnp.where(diagonal(columns.shape[0], n), tiled, 0.0).astype(jnp.bfloat16)

def diagonal(rows, n):
    wide = TILE * n
    return lax.broadcasted_iota(jnp.int32, (rows, wide), 1) // n == lax.broadcasted_iota(jnp.int32, (rows, wide), 0) % TILE

def mm(a, b):
    return jnp.dot(a, b, preferred_element_type=jnp.float32)

def mt(a, b):
    return lax.dot_general(a, b, (((1,), (1,)), ((), ())), preferred_element_type=jnp.float32)

WINDOW = 512
PEAK = 1.1e15


def taking(microseconds, moved=0):
    return pl.CostEstimate(flops=int(microseconds * 1e-6 * PEAK), bytes_accessed=int(moved), transcendentals=0)


def first_window(bounds, row, m, span, window):
    first, last = bounds[row, m], bounds[row, m + 1]
    base = lax.div(first, 128) * 128
    count = jnp.where(last > first, lax.div(last - base + window - 1, window), 0)
    return first, last, base, count


def inside(at, low, high, window):
    here = at + lax.broadcasted_iota(jnp.int32, (window, 128), 0)
    return jnp.where((here >= low) & (here < high), 1.0, 0.0).astype(jnp.bfloat16)


def grouped_sum(bounds, slots, m, span, window, left_at, right_at, acc, start):
    lefts, rights, more = [], [], []
    for s in range(slots):
        first, last, base, count = first_window(bounds, s, m, span, window)
        at = pl.multiple_of(jnp.minimum(base, span - window), 128)
        keep = inside(at, first, last, window)
        lefts.append(left_at(s, at, keep))
        rights.append(right_at(s, at, keep))
        more.append((last, base, count))
    total = mm(jnp.concatenate(lefts, 1), jnp.concatenate(rights, 0))
    acc[...] = total if start is None else total + start[0]
    for s, (last, base, count) in enumerate(more):

        def one(i, _):
            want = base + i * window
            at = pl.multiple_of(jnp.minimum(want, span - window), 128)
            keep = inside(at, want, last, window)
            acc[...] += mm(left_at(s, at, keep), right_at(s, at, keep))
            return 0

        lax.fori_loop(1, count, one, 0)


def grad_in_kernel(bounds, *refs, slots, begun, halves):
    rows, d, rest = refs[:slots], refs[slots : 2 * slots], refs[2 * slots : -2]
    out, acc = refs[-2:]
    wide, _, unit, bf = rows[0].shape
    span, chan = d[0].shape
    window = min(WINDOW, span)

    def left_at(s, at, keep):
        block = rows[s][pl.ds(lax.div(at, unit), window // unit), 0]
        return jnp.transpose(block.reshape(window, bf))

    def right_at(s, at, keep):
        return d[s][pl.ds(at, window), :] * jnp.concatenate([keep] * (chan // 128), 1)

    grouped_sum(bounds, slots, pl.program_id(1), span, window, left_at, right_at, acc, rest[0] if begun else None)
    if halves:
        other = rest[-1]
        lanes = chan // 128
        for j in range(lanes):
            out[0, pl.ds(j * 2, bf, stride=2 * lanes), :] = acc[:, j * 128 : (j + 1) * 128]
            out[0, pl.ds(j * 2 + 1, bf, stride=2 * lanes), :] = other[0, :, j * 128 : (j + 1) * 128]
    else:
        out[0] = acc[...]


def slot_spec(array, index, bf):
    return pl.BlockSpec((array.shape[0], 1, array.shape[2], bf), lambda f, m, b: (0, index, 0, f))


def side_spec(array, chan, side):
    return pl.BlockSpec((array.shape[0], chan), lambda f, m, b: (0, side))


def feature_block(rows):
    wide, _, unit, width = rows[0][0].shape
    return max(128, min(1024, (1 << 20) // (wide * unit)))


def grad_in(bounds, rows, d, mods, chan, side, start=None, other=None):
    width = rows[0][0].shape[3]
    bf = feature_block(rows)
    span, slots = d[0].shape[0], len(d)
    plain = pl.BlockSpec((1, bf, chan), lambda f, m, b: (m, f, 0))
    ins = [slot_spec(array, index, bf) for array, index in rows] + [side_spec(x, chan, side) for x in d]
    args = [array for array, _ in rows] + list(d)
    for extra in (start, other):
        if extra is not None:
            ins.append(plain)
            args.append(extra)
    if other is not None:
        out_shape = jax.ShapeDtypeStruct((mods, width * 2 * chan // 128, 128), jnp.float32)
        out_spec = pl.BlockSpec((1, bf * 2 * chan // 128, 128), lambda f, m, b: (m, f, 0))
    else:
        out_shape = jax.ShapeDtypeStruct((mods, width, chan), jnp.float32)
        out_spec = plain
    return pl.pallas_call(
        functools.partial(grad_in_kernel, slots=slots, begun=start is not None, halves=other is not None),
        grid_spec=pltpu.PrefetchScalarGridSpec(
            num_scalar_prefetch=1,
            grid=(width // bf, mods),
            in_specs=ins,
            out_specs=out_spec,
            scratch_shapes=[pltpu.VMEM((bf, chan), jnp.float32)],
        ),
        out_shape=out_shape,
        compiler_params=pltpu.CompilerParams(vmem_limit_bytes=56 << 20),
        cost_estimate=taking(6 * slots + 6),
    )(bounds, *args)


def grad_out_kernel(bounds, *refs, slots):
    cot, gated, out = refs[:slots], refs[slots : 2 * slots], refs[-1]
    wide, _, unit, bf = cot[0].shape
    span, chan = gated[0].shape
    window = min(WINDOW, span)

    def left_at(s, at, keep):
        return jnp.transpose(gated[s][pl.ds(at, window), :] * jnp.concatenate([keep] * (chan // 128), 1))

    def right_at(s, at, keep):
        return cot[s][pl.ds(lax.div(at, unit), window // unit), 0].reshape(window, bf)

    grouped_sum(bounds, slots, pl.program_id(1), span, window, left_at, right_at, out.at[0], None)


def grad_out(bounds, cot, gated, mods, chan, side):
    width = cot[0][0].shape[3]
    bf = feature_block(cot)
    slots = len(gated)
    return pl.pallas_call(
        functools.partial(grad_out_kernel, slots=slots),
        grid_spec=pltpu.PrefetchScalarGridSpec(
            num_scalar_prefetch=1,
            grid=(width // bf, mods),
            in_specs=[slot_spec(array, index, bf) for array, index in cot] + [side_spec(x, chan, side) for x in gated],
            out_specs=pl.BlockSpec((1, chan, bf), lambda f, m, b: (m, 0, f)),
        ),
        out_shape=jax.ShapeDtypeStruct((mods, chan, width), jnp.float32),
        compiler_params=pltpu.CompilerParams(vmem_limit_bytes=56 << 20),
        cost_estimate=taking(6 * slots + 4),
    )(bounds, *[array for array, _ in cot], *gated)


def fwd_kernel(lr, dtw, dtb, cf, ct, u, alog, skip, gate, dgated, gated, dy, dgate, starts, h_s, dt_s, du_s, y_s, bd_s, hb_s):
    span, chan = u.shape
    n = alog.shape[0]
    @pl.when(pl.program_id(0) == 0)
    def _():
        h_s[...] = jnp.zeros_like(h_s)
    rate = -jnp.exp(alog[...]) * LOG2E
    dt = softplus(mm(lr[...], dtw[...]) + dtb[...])
    uf = u[...].astype(jnp.float32)
    dt_s[...] = dt
    du_s[...] = dt * uf
    starts[0] = h_s[...]
    bd_s[...] = spread(cf[:, n:], n)
    block = FU * TILE
    def reduce(g):
        for k in range(FU):
            t0 = pl.multiple_of(g * block + k * TILE, TILE)
            y_s[pl.ds(t0, TILE), :] = mm(bd_s[pl.ds(t0, TILE), :], hb_s[pl.ds(pl.multiple_of(t0 * n, TILE * n), TILE * n), :])
    def group(g, h):
        c = pltpu.roll(ct[:n, :], span - g * block, 1)
        reduce(jnp.maximum(g - 1, 0))
        for j in range(block):
            t = g * block + j
            e = jnp.exp2(dt_s[pl.ds(t, 1), :] * rate)
            h = e * h + du_s[pl.ds(t, 1), :] * c[:, j:j+1]
            hb_s[pl.ds(pl.multiple_of(t * n, n), n), :] = h.astype(jnp.bfloat16)
        return h
    h_s[...] = lax.fori_loop(0, span // block, group, h_s[...])
    reduce(span // block - 1)
    y = (y_s[...] + skip[...] * uf).astype(jnp.bfloat16).astype(jnp.float32)
    g = gate[...]
    sig = jax.nn.sigmoid(g)
    silu = g * sig
    dg = dgated[...]
    gated[...] = (y * silu).astype(jnp.bfloat16)
    dy[...] = (dg * silu).astype(jnp.bfloat16)
    dgate[...] = (dg * y * sig * (1.0 + g * (1.0 - sig))).astype(jnp.bfloat16)

def scan_forward(lr, dtw, dtb, cf, ct, u, alog, skip, gate, dgated, span=SPAN):
    rows, chan = u.shape
    n = alog.shape[0]
    rank = lr.shape[1]
    steps = rows // span
    full = lambda a: pl.BlockSpec(a.shape, lambda i: (0,) * a.ndim)
    tok = lambda w: pl.BlockSpec((span, w), lambda i: (i, 0))
    return pl.pallas_call(
        fwd_kernel, grid=(steps,),
        in_specs=[tok(rank), full(dtw), full(dtb), tok(2*n), pl.BlockSpec((2*n, span), lambda i: (0, i)), tok(chan), full(alog), full(skip), tok(chan), tok(chan)],
        out_specs=[tok(chan)] * 3 + [pl.BlockSpec((1, n, chan), lambda i: (i, 0, 0))],
        out_shape=[jax.ShapeDtypeStruct((rows, chan), jnp.bfloat16)] * 3 + [jax.ShapeDtypeStruct((steps, n, chan), jnp.float32)],
        scratch_shapes=[pltpu.VMEM((n, chan), jnp.float32)] + [pltpu.VMEM((span, chan), jnp.float32)] * 3 + [pltpu.VMEM((span, TILE * n), jnp.bfloat16), pltpu.VMEM((span * n, chan), jnp.bfloat16)],
        compiler_params=pltpu.CompilerParams(vmem_limit_bytes=32 << 20),
        cost_estimate=taking(13 * rows / 1024),
    )(lr, dtw, dtb, cf, ct, u, alog, skip, gate, dgated)

def bwd_kernel(lr, dtw, dtb, cf, ct, u, alog, skip, dy, starts, dpre, dval, dlow, din, dout, galog, gskip, gbias, gdtw, lam_s, dt_s, du_s, dyf_s, hp_s, st_s, th_s, bd_s, hb_s, gb_s):
    span, chan = u.shape
    n = alog.shape[0]
    @pl.when(pl.program_id(0) == 0)
    def _():
        lam_s[...] = jnp.zeros_like(lam_s)
        galog[...] = jnp.zeros_like(galog)
        gskip[...] = jnp.zeros_like(gskip)
        gbias[...] = jnp.zeros_like(gbias)
        gdtw[...] = jnp.zeros_like(gdtw)
    decay = -jnp.exp(alog[...])
    rate = decay * LOG2E
    pre = mm(lr[...], dtw[...]) + dtb[...]
    dt = softplus(pre)
    uf = u[...].astype(jnp.float32)
    dyf = dy[...].astype(jnp.float32)
    dt_s[...] = dt
    du_s[...] = dt * uf
    dyf_s[...] = dyf
    bd_s[...] = spread(cf[:, :n], n)
    mask = diagonal(TILE, n)
    ones = mask.astype(jnp.bfloat16)
    block = FU * TILE
    def reduce_h(g):
        for k in range(FU):
            t0 = pl.multiple_of(g * block + k * TILE, TILE)
            cross = mt(dy[pl.ds(t0, TILE), :], hb_s[pl.ds(pl.multiple_of(t0 * n, TILE * n), TILE * n), :])
            dout[0, pl.ds(g * FU + k, 1), :] = jnp.sum(jnp.where(mask, cross, 0.0), axis=0, keepdims=True)
    def again(g, h):
        c = pltpu.roll(ct[:n, :], span - g * block, 1)
        reduce_h(jnp.maximum(g - 1, 0))
        for j in range(block):
            t = g * block + j
            hp_s[t] = h
            e = jnp.exp2(dt_s[pl.ds(t, 1), :] * rate)
            h = e * h + du_s[pl.ds(t, 1), :] * c[:, j:j+1]
            hb_s[pl.ds(pl.multiple_of(t * n, n), n), :] = h.astype(jnp.bfloat16)
        return h
    lax.fori_loop(0, span // block, again, starts[0])
    reduce_h(span // block - 1)
    back = BU * TILE
    per = span // back
    def reduce_lam(g):
        for k in range(BU - 1, -1, -1):
            t0 = pl.multiple_of(g * back + k * TILE, TILE)
            wide = pl.ds(pl.multiple_of(t0 * n, TILE * n), TILE * n)
            lam16 = hb_s[wide, :]
            st_s[pl.ds(t0, TILE), :] = mm(ones, gb_s[wide, :])
            th_s[pl.ds(t0, TILE), :] = mm(bd_s[pl.ds(t0, TILE), :], lam16)
            cross = mt(du_s[pl.ds(t0, TILE), :].astype(jnp.bfloat16), lam16)
            din[0, pl.ds(g * BU + k, 1), :] = jnp.sum(jnp.where(mask, cross, 0.0), axis=0, keepdims=True)
    def group(q, state):
        carry, gdec = state
        g = per - 1 - q
        c = pltpu.roll(ct[n:, :], span - g * back, 1)
        reduce_lam(jnp.minimum(g + 1, per - 1))
        for j in range(back - 1, -1, -1):
            t = g * back + j
            here = pl.ds(pl.multiple_of(t * n, n), n)
            d = dt_s[pl.ds(t, 1), :]
            lam = carry + dyf_s[pl.ds(t, 1), :] * c[:, j:j+1]
            carry = lam * jnp.exp2(d * rate)
            grow = carry * hp_s[t]
            gdec = gdec + grow * d
            hb_s[here, :] = lam.astype(jnp.bfloat16)
            gb_s[here, :] = (grow * decay).astype(jnp.bfloat16)
        return carry, gdec
    carry, gdec = lax.fori_loop(0, per, group, (lam_s[...], jnp.zeros_like(decay)))
    reduce_lam(0)
    lam_s[...] = carry
    galog[...] += gdec * decay
    gskip[...] += jnp.sum(dyf * uf, axis=0, keepdims=True)
    thru = th_s[...]
    dp = ((st_s[...] + thru * uf) * jax.nn.sigmoid(pre)).astype(jnp.bfloat16)
    dpre[...] = dp
    dval[...] = thru * dt + skip[...] * dyf
    gbias[...] += jnp.sum(dp.astype(jnp.float32), axis=0, keepdims=True)
    dlow[...] = mt(dp, dtw[...])
    gdtw[...] += lax.dot_general(lr[...], dp, (((0,), (0,)), ((), ())), preferred_element_type=jnp.float32)

def scan_backward(lr, dtw, dtb, cf, ct, u, alog, skip, dy, starts, span=SPAN):
    rows, chan = u.shape
    n = alog.shape[0]
    rank = lr.shape[1]
    steps = rows // span
    full = lambda a: pl.BlockSpec(a.shape, lambda i: (0,) * a.ndim)
    tok = lambda w: pl.BlockSpec((span, w), lambda i: (steps - 1 - i, 0))
    ctok = pl.BlockSpec((2*n, span), lambda i: (0, steps - 1 - i))
    ptok = pl.BlockSpec((1, span // TILE, TILE * n), lambda i: (steps - 1 - i, 0, 0))
    f = lambda *s: jax.ShapeDtypeStruct(s, jnp.float32)
    outs = [jax.ShapeDtypeStruct((rows, chan), jnp.bfloat16), f(rows, chan), f(rows, rank), f(steps, span // TILE, TILE * n), f(steps, span // TILE, TILE * n), f(n, chan), f(1, chan), f(1, chan), f(rank, chan)]
    return pl.pallas_call(
        bwd_kernel, grid=(steps,),
        in_specs=[tok(rank), full(dtw), full(dtb), tok(2*n), ctok, tok(chan), full(alog), full(skip), tok(chan), pl.BlockSpec((1, n, chan), lambda i: (steps - 1 - i, 0, 0))],
        out_specs=[tok(chan), tok(chan), tok(rank), ptok, ptok] + [full(o) for o in outs[5:]],
        out_shape=outs,
        scratch_shapes=[pltpu.VMEM((n, chan), jnp.float32)] + [pltpu.VMEM((span, chan), jnp.float32)] * 3 + [pltpu.VMEM((span, n, chan), jnp.float32)] + [pltpu.VMEM((span, chan), jnp.float32)] * 2 + [pltpu.VMEM((span, TILE * n), jnp.bfloat16)] + [pltpu.VMEM((span * n, chan), jnp.bfloat16)] * 2,
        compiler_params=pltpu.CompilerParams(vmem_limit_bytes=32 << 20),
        cost_estimate=taking(36 * rows / 1024),
    )(lr, dtw, dtb, cf, ct, u, alog, skip, dy, starts)


def shifted(block, before, back):
    if back == 0:
        return block
    rows = block.shape[0]
    return jnp.concatenate([before[8 - back :], block[: rows - back]], 0)


def masked_sum(x, masks, weights, product):
    total = None
    for m in range(weights[0].shape[0]):
        held = x * masks[:, m : m + 1]
        parts = [product(held, w[m]) for w in weights]
        total = parts if total is None else [t + p for t, p in zip(total, parts)]
    return total


def enter_kernel(rows, masks, w, cw, cb, xp, conv_in, gate_in, pre_act, conv_out, part, tail):
    @pl.when(pl.program_id(0) == 0)
    def _():
        tail[...] = jnp.zeros_like(tail)

    taps = cw.shape[0]
    ax, az = masked_sum(rows[...], masks[...], (w.at[0], w.at[1]), mm)
    before = tail[...]
    pre = cb[...]
    for k in range(taps):
        pre = pre + cw[k : k + 1] * shifted(ax, before, taps - 1 - k)
    tail[...] = ax[-8:]
    out = (pre * jax.nn.sigmoid(pre)).astype(jnp.bfloat16)
    conv_in[...] = ax
    gate_in[...] = az
    pre_act[...] = pre
    conv_out[...] = out
    part[...] = mm(out, xp[...])


def whole_spec(a):
    return pl.BlockSpec(a.shape, lambda i: (0,) * len(a.shape))


def enter(rows, masks, w, cw, cb, xp, block):
    span, width = rows.shape
    chan, small = xp.shape
    tok = lambda w: pl.BlockSpec((block, w), lambda i: (i, 0))
    f = lambda w, t=jnp.float32: jax.ShapeDtypeStruct((span, w), t)
    return pl.pallas_call(
        enter_kernel,
        grid=(span // block,),
        in_specs=[tok(width), tok(masks.shape[1])] + [whole_spec(a) for a in (w, cw, cb, xp)],
        out_specs=[tok(chan)] * 4 + [tok(small)],
        out_shape=[f(chan), f(chan), f(chan), f(chan, jnp.bfloat16), f(small)],
        scratch_shapes=[pltpu.VMEM((8, chan), jnp.float32)],
        compiler_params=pltpu.CompilerParams(vmem_limit_bytes=56 << 20),
        cost_estimate=taking(20),
    )(rows, masks, w, cw, cb, xp)


def apply_kernel(masks, *refs, turned):
    *inputs, w, out = refs
    total = None
    for k, x in enumerate(inputs):
        (part,) = masked_sum(x[...], masks[...], (w.at[k],), mt if turned else mm)
        total = part if total is None else total + part
    out[...] = total.astype(out.dtype)


def apply(masks, inputs, w, turned, dtype, block):
    span = masks.shape[0]
    width = w.shape[2 if turned else 3]
    tok = lambda c: pl.BlockSpec((block, c), lambda i: (i, 0))
    return pl.pallas_call(
        functools.partial(apply_kernel, turned=turned),
        grid=(span // block,),
        in_specs=[tok(masks.shape[1])] + [tok(x.shape[1]) for x in inputs] + [whole_spec(w)],
        out_specs=tok(width),
        out_shape=jax.ShapeDtypeStruct((span, width), dtype),
        compiler_params=pltpu.CompilerParams(vmem_limit_bytes=56 << 20),
        cost_estimate=taking(20 * w.size / 6e6),
    )(masks, *inputs, w)


def leave_kernel(dval, dsmall, xp, pre_act, conv_in, prev_in, conv_out, cw, d_conv_in, grad_taps, grad_bias, grad_x, head):
    i = pl.program_id(0)
    steps = pl.num_programs(0)

    @pl.when(i == 0)
    def _():
        head[...] = jnp.zeros_like(head)
        grad_taps[...] = jnp.zeros_like(grad_taps)
        grad_bias[...] = jnp.zeros_like(grad_bias)
        grad_x[...] = jnp.zeros_like(grad_x)

    taps = cw.shape[0]
    d_out = (dval[...] + mt(dsmall[...], xp[...])).astype(jnp.bfloat16).astype(jnp.float32)
    pre = pre_act[...]
    sig = jax.nn.sigmoid(pre)
    d_pre = d_out * sig * (1.0 + pre * (1.0 - sig))
    before = jnp.where(i == steps - 1, 0.0, prev_in[...])
    held = conv_in[...]
    rows = held.shape[0]
    after = head[...]
    total = None
    for k in range(taps):
        back = taps - 1 - k
        grad_taps[k : k + 1] += jnp.sum(d_pre * shifted(held, before, back), axis=0, keepdims=True)
        moved = d_pre if back == 0 else jnp.concatenate([d_pre[back:], after[:back]], 0)
        term = cw[k : k + 1] * moved
        total = term if total is None else total + term
    head[...] = d_pre[:8]
    d_conv_in[...] = total.astype(jnp.bfloat16)
    grad_bias[...] += jnp.sum(d_pre, axis=0, keepdims=True)
    grad_x[...] += lax.dot_general(conv_out[...], dsmall[...], (((0,), (0,)), ((), ())), preferred_element_type=jnp.float32)


def leave(dval, dsmall, xp, pre_act, conv_in, conv_out, cw, block):
    span, chan = pre_act.shape
    steps = span // block
    taps, small = cw.shape[0], xp.shape[1]
    tok = lambda w: pl.BlockSpec((block, w), lambda i: (steps - 1 - i, 0))
    prev = pl.BlockSpec((8, chan), lambda i: (jnp.maximum((steps - 1 - i) * (block // 8) - 1, 0), 0))
    f = lambda *s: jax.ShapeDtypeStruct(s, jnp.float32)
    outs = [jax.ShapeDtypeStruct((span, chan), jnp.bfloat16), f(taps, chan), f(1, chan), f(chan, small)]
    return pl.pallas_call(
        leave_kernel,
        grid=(steps,),
        in_specs=[tok(chan), tok(small), whole_spec(xp), tok(chan), tok(chan), prev, tok(chan), whole_spec(cw)],
        out_specs=[tok(chan)] + [whole_spec(o) for o in outs[1:]],
        out_shape=outs,
        scratch_shapes=[pltpu.VMEM((8, chan), jnp.float32)],
        compiler_params=pltpu.CompilerParams(vmem_limit_bytes=56 << 20),
        cost_estimate=taking(8),
    )(dval, dsmall, xp, pre_act, conv_in, conv_in, conv_out, cw)


def sort_kernel(start, rank, *refs):
    inputs, out = refs[:-1], refs[-1]
    rows, span = out.shape[0], inputs[0].shape[0]
    first = start[0] + pl.program_id(0) * rows
    here = lax.broadcasted_iota(jnp.int32, (rows, span), 0) + first
    choose = jnp.where(rank[...] == here, 1.0, 0.0).astype(jnp.bfloat16)
    at = 0
    for x in inputs:
        out[:, at : at + x.shape[1]] = mm(choose, x[...]).astype(out.dtype)
        at += x.shape[1]


def sort_rows(start, rank, inputs, rows, block):
    span = inputs[0].shape[0]
    width = sum(x.shape[1] for x in inputs)
    return pl.pallas_call(
        sort_kernel,
        grid_spec=pltpu.PrefetchScalarGridSpec(
            num_scalar_prefetch=1,
            grid=(rows // block,),
            in_specs=[pl.BlockSpec((1, span), lambda i, s: (0, 0))]
            + [pl.BlockSpec((span, x.shape[1]), lambda i, s: (0, 0)) for x in inputs],
            out_specs=pl.BlockSpec((block, width), lambda i, s: (i, 0)),
        ),
        out_shape=jax.ShapeDtypeStruct((rows, width), inputs[0].dtype),
        compiler_params=pltpu.CompilerParams(vmem_limit_bytes=56 << 20),
        cost_estimate=taking(2 + 2e-9 * rows * span * width),
    )(start, rank, *inputs)


def contract(left, right, left_dim, right_dim):
    return lax.dot_general(
        left, right, (((left_dim,), (right_dim,)), ((), ())), preferred_element_type=jnp.float32
    )


def own(array, dim, size):
    return lax.dynamic_slice_in_dim(array, lax.axis_index("wide") * size, size, dim)


def pick(array, index, dim=0):
    return lax.dynamic_index_in_dim(array, index, dim, False)


def cross(array, k):
    return lax.ppermute(array, "wide", [(i, i ^ k) for i in range(lax.axis_size("wide"))])


def gather_wide(shard, early, late):
    if lax.axis_size("wide") != 8:
        return lax.all_gather(shard, "wide", axis=0), early(), late()
    half = shard.shape[0] // 2
    by_x, by_y, pair = cross(shard, 2), cross(shard, 4), cross(shard, 1)
    early, by_x, by_y, pair = lax.optimization_barrier((early(), by_x, by_y, pair))
    far = (cross(by_y[:half], 2), cross(by_x[half:], 4))
    pair_x, pair_y = cross(by_x, 1), cross(by_y, 1)
    late, *far = lax.optimization_barrier((late(),) + far)
    far = jnp.concatenate(far, 0)
    blocks = [shard, pair, by_x, pair_x, by_y, pair_y, far, cross(far, 1)]
    here = lax.axis_index("wide")
    whole = jnp.zeros((8,) + shard.shape, shard.dtype)
    for k, block in enumerate(blocks):
        whole = lax.dynamic_update_index_in_dim(whole, block, here ^ k, 0)
    return whole, early, late


def sum_wide(part, work):
    if lax.axis_size("wide") != 8:
        return lax.psum(part, "wide"), work()
    half = part.shape[0] // 2
    core = lax.axis_index("wide") % 2
    mine = lax.dynamic_slice_in_dim(part, core * half, half, 0)
    other = lax.dynamic_slice_in_dim(part, (1 - core) * half, half, 0)
    mine = mine + cross(other, 1)
    sent = mine.astype(jnp.bfloat16)
    beside, *came = lax.optimization_barrier((work(),) + tuple(cross(sent, k) for k in (2, 4, 6)))
    total = mine
    for block in came:
        total = total + block.astype(jnp.float32)
    other = cross(total, 1)
    return jnp.where(core == 0, jnp.concatenate([total, other], 0), jnp.concatenate([other, total], 0)), beside


def scatter_wide(part, work):
    if lax.axis_size("wide") != 8:
        return lax.psum_scatter(part, "wide", scatter_dimension=0, tiled=True).astype(jnp.float32), work()
    here = lax.axis_index("wide")
    core, chip = here % 2, here // 2
    view = part.reshape(4, 2, part.shape[0] // 8, part.shape[1])
    mine = pick(view, core, 1).astype(jnp.float32) + cross(pick(view, 1 - core, 1), 1).astype(jnp.float32)
    came = tuple(cross(pick(mine, chip ^ (k // 2)).astype(jnp.bfloat16), k) for k in (2, 4, 6))
    beside, *came = lax.optimization_barrier((work(),) + came)
    total = pick(mine, chip)
    for block in came:
        total = total + block.astype(jnp.float32)
    return total, beside


def after(value, *first):
    return lax.optimization_barrier((value,) + first)[0]


def hop(rising, falling):
    return (
        lax.ppermute(rising, "row", [(0, 1), (1, 2), (2, 3)]),
        lax.ppermute(falling, "row", [(1, 0), (2, 1), (3, 2)]),
    )


def arrange_near(hops):
    return jnp.where(lax.axis_index("row") == 0, hops[0][1], hops[0][0])


def arrange_middle(hops):
    return hops[1][0] + hops[1][1]


def arrange_last(hops):
    here = lax.axis_index("row")
    return jnp.where(here == 3, hops[2][0], jnp.where(here == 0, hops[2][1], hops[0][1]))


def arrange(block, hops):
    return [block, arrange_near(hops), arrange_middle(hops), arrange_last(hops)]


def sum_row(part):
    if lax.axis_size("row") != 4:
        return lax.psum(part, "row")
    for k in (1, 2):
        part = part + lax.ppermute(part, "row", [(i, i ^ k) for i in range(4)])
    return part


def sum_row_low(part):
    if lax.axis_size("row") != 4:
        return lax.psum(part.astype(jnp.bfloat16), "row").astype(jnp.float32)
    for k in (1, 2):
        sent = lax.ppermute(part.astype(jnp.bfloat16), "row", [(i, i ^ k) for i in range(4)])
        part = part + sent.astype(jnp.float32)
    return part


def share_wide(part):
    count = lax.axis_size("wide")
    if count != 8:
        return lax.psum_scatter(part, "wide", scatter_dimension=0, tiled=True)
    for k in (1, 2, 4):
        part = part + cross(part, k)
    return own(part, 0, part.shape[0] // count)


def row_order():
    count = lax.axis_size("row")
    here = lax.axis_index("row")
    if count != 4:
        return [lax.rem(here + s, count) for s in range(count)]
    near = jnp.where(here == 0, 1, here - 1)
    last = jnp.where(here == 3, 0, jnp.where(here == 0, 3, here + 1))
    return [here, near, lax.rem(here + 2, 4), last]


def others(array, order):
    return jnp.stack([pick(array, q) for q in order[1:]], 0)


def gather_ordered(block, order):
    whole = lax.all_gather(block, "row", axis=0)
    return [block] + [pick(whole, q) for q in order[1:]]


def sorted_places(ids, mods):
    one = (ids[:, None] == jnp.arange(mods, dtype=ids.dtype)[None]).astype(jnp.int32)
    before = jnp.cumsum(one, 0)
    total = before[-1]
    first = jnp.cumsum(total) - total
    return jnp.sum(one * (before - 1 + first[None]), 1)[None]


def group_bounds(ids, mods):
    count = jnp.sum((ids[:, None] == jnp.arange(mods, dtype=ids.dtype)).astype(jnp.int32), 0)
    return jnp.concatenate([jnp.zeros((1,), jnp.int32), jnp.cumsum(count)], 0)


def local(
    hidden,
    modality,
    norm_gain,
    in_proj,
    conv_weight,
    conv_bias,
    x_proj_dt,
    x_proj_bc,
    dt_proj,
    dt_bias,
    a_log,
    skip_weight,
    out_proj,
    cotangent,
):
    shard_rows, width = hidden.shape
    mods = in_proj.shape[0]
    chan = in_proj.shape[3]
    taps = conv_weight.shape[0]
    n = a_log.shape[0]
    rank = dt_proj.shape[0]
    row_count = lax.axis_size("row")
    residual = hidden.astype(jnp.float32)
    inv_rms = lax.rsqrt(jnp.mean(residual * residual, axis=-1, keepdims=True) + EPS)
    gain_vec = norm_gain.astype(jnp.float32)
    normed = (residual * inv_rms * gain_vec).astype(jnp.bfloat16)
    lanes = jnp.pad(modality.astype(jnp.bfloat16)[None], ((0, 15), (0, width - shard_rows)))
    conv_taps = conv_weight.astype(jnp.float32)
    w_out = out_proj[None]

    def small_slices():
        x_proj = jnp.concatenate([own(x_proj_dt, 0, chan), own(x_proj_bc, 0, chan)], 1)
        return x_proj, own(dt_proj, 1, chan), own(dt_bias, 0, chan)[None], own(a_log, 1, chan), own(skip_weight, 0, chan)[None]

    gathered, w_in, (x_proj, dtw, dtb, alog, skip) = gather_wide(
        jnp.concatenate([normed, lanes], 0), lambda: jnp.transpose(in_proj, (2, 0, 1, 3)), small_slices
    )
    rows = gathered[:, :shard_rows].reshape(-1, width)
    ids = gathered[:, shard_rows, :shard_rows].astype(jnp.int32).reshape(-1)
    masks = (ids[:, None] == jnp.arange(128, dtype=ids.dtype)[None]).astype(jnp.bfloat16)
    span_rows = rows.shape[0]
    block = min(256, span_rows)
    order = row_order()
    slot = jnp.arange(row_count, dtype=jnp.int32)[:, None] == lax.axis_index("row")
    whole = jnp.zeros((1,), jnp.int32)
    chunk = lax.axis_index("wide").astype(jnp.int32)[None] * shard_rows
    conv_in, gate_in, pre_act, conv_out, part = enter(
        rows, masks, w_in, conv_taps, conv_bias.astype(jnp.float32)[None], x_proj, block
    )
    places = sorted_places(ids, mods)

    def sort_chunk():
        return sort_rows(chunk, places, (rows,), shard_rows, shard_rows)

    cot_gathered, part, rows_chunk = gather_wide(after(cotangent, rows), lambda: part, sort_chunk)
    cot_rows = cot_gathered.reshape(-1, width)
    rows_near = lax.all_gather(rows_chunk, "row", axis=0)

    def first_work():
        cot_chunk = sort_rows(chunk, places, (cot_rows,), shard_rows, shard_rows)
        return cot_chunk, apply(masks, (cot_rows,), w_out, True, jnp.float32, block)

    small, (cot_chunk, d_gated) = sum_wide(part, first_work)
    small, rows_near = lax.optimization_barrier((small, rows_near))
    cot_near = lax.all_gather(cot_chunk, "row", axis=0)
    rows_far = lax.all_gather(others(rows_near, order), "wide", axis=0)
    low_rank = small[:, :rank].astype(jnp.bfloat16)
    coefs = small[:, rank:]
    gated, d_y, d_gate_in, starts = scan_forward(
        low_rank, dtw, dtb, coefs, coefs.T, conv_out, alog, skip, gate_in, d_gated
    )
    line = row_count == 4
    gates = sort_rows(whole, places, (gated, d_gate_in), span_rows, block)
    d_y, gates = lax.optimization_barrier((d_y, gates))
    gate_hops = [hop(gates, gates)] if line else []
    d_pre_step, d_value, d_low_part, d_in, d_out, grad_alog, grad_skip, grad_bias, grad_wdtp = scan_backward(
        low_rank, dtw, dtb, coefs, coefs.T, conv_out, alog, skip, d_y, starts
    )
    d_part = jnp.concatenate([d_low_part, d_in.reshape(span_rows, n), d_out.reshape(span_rows, n)], 1)
    if line:
        d_part, cot_near, gate_hops[0] = lax.optimization_barrier((d_part, cot_near, gate_hops[0]))
        gate_hops.append(hop(*gate_hops[0]))
    cot_far = lax.all_gather(others(cot_near, order), "wide", axis=0)
    d_small, projected = sum_wide(
        d_part, lambda: apply(masks, (after(gated, d_part),), w_out, False, jnp.bfloat16, block)
    )
    d_small = d_small.astype(jnp.bfloat16)
    if line:
        d_small, projected, gate_hops[1] = lax.optimization_barrier((d_small, projected, gate_hops[1]))
        gate_hops.append(hop(*gate_hops[1]))
    d_conv_in, grad_taps, grad_cbias, grad_x = leave(
        d_value, d_small, x_proj, pre_act, conv_in, conv_out, conv_taps, block
    )
    conv_sorted = sort_rows(whole, places, (d_conv_in,), span_rows, block)
    d_conv_in, conv_sorted = lax.optimization_barrier((d_conv_in, conv_sorted))
    conv_hops = [hop(conv_sorted, conv_sorted)] if line else []

    def second_work():
        part = apply(masks, (d_conv_in, d_gate_in), w_in, True, jnp.bfloat16, block)
        rows_sorted = sort_rows(whole, places, (after(rows, d_conv_in),), span_rows, block)
        cot_sorted = sort_rows(whole, places, (after(cot_rows, d_conv_in),), span_rows, block)
        return part, rows_sorted, cot_sorted

    projected, (normed_part, rows_sorted, cot_sorted) = scatter_wide(projected, second_work)
    output = (residual + projected).astype(jnp.bfloat16)
    bounds = sum_row(jnp.where(slot, group_bounds(after(ids, d_small), mods)[None], 0))
    bounds = jnp.stack([pick(bounds, q) for q in order], 0)
    if line:
        normed_part, gate_hops[2], conv_hops[0] = lax.optimization_barrier((normed_part, gate_hops[2], conv_hops[0]))
        conv_hops.append(hop(*conv_hops[0]))
        gates = arrange(gates, gate_hops)
    else:
        gates = gather_ordered(gates, order)
        conv_all = gather_ordered(conv_sorted, order)
    apart = lambda a: a.reshape(span_rows // shard_rows, 1, shard_rows, width)
    far = range(row_count - 1)
    rows_slots = [(apart(rows_sorted), 0)] + [(rows_far, s) for s in far]
    cot_slots = [(apart(cot_sorted), 0)] + [(cot_far, s) for s in far]
    d_normed, grad_z = scatter_wide(normed_part, lambda: grad_in(bounds, rows_slots, gates, mods, chan, 1))
    weighted = gain_vec * d_normed
    grad_hidden = (
        cotangent.astype(jnp.float32)
        + inv_rms * weighted
        - residual * inv_rms * inv_rms * inv_rms * jnp.mean(weighted * residual, axis=-1, keepdims=True)
    )
    g_gain = sum_row(share_wide(jnp.sum(d_normed * residual * inv_rms, 0)))

    if line:
        grad_z, conv_hops[1] = lax.optimization_barrier((grad_z, conv_hops[1]))
        conv_hops.append(hop(*conv_hops[1]))
        early = [conv_sorted, arrange_near(conv_hops), arrange_middle(conv_hops)]
    else:
        early = conv_all[:-1]
    grad_x_most = grad_in(bounds[:-1], rows_slots[:-1], early, mods, chan, 0)
    grad_wout = grad_out(bounds, cot_slots, gates, mods, chan, 0)
    if line:
        grad_x_most, grad_wout, conv_hops[2] = lax.optimization_barrier((grad_x_most, grad_wout, conv_hops[2]))
        last = arrange_last(conv_hops)
    else:
        last = conv_all[-1]
    grad_win = grad_in(bounds[-1:], rows_slots[-1:], [last], mods, chan, 0, grad_x_most, grad_z)
    grad_win = grad_win.reshape(mods, width, chan // 128, 2, 128).transpose(0, 1, 3, 2, 4).reshape(mods, width, 2, chan)
    small_grads = (grad_taps, grad_cbias[0], grad_x, grad_wdtp, grad_bias[0], grad_alog, grad_skip[0])
    flat = after(jnp.concatenate([g.reshape(-1) for g in small_grads]).reshape(-1, 128), grad_z)
    flat = sum_row_low(flat).reshape(-1)
    summed, at = [], 0
    for g in small_grads:
        summed.append(flat[at : at + g.size].reshape(g.shape))
        at += g.size
    g_taps, g_cbias, g_x, g_wdtp, g_bias, g_alog, g_skip = summed
    return (
        output,
        grad_hidden,
        g_gain,
        grad_win,
        g_taps,
        g_cbias,
        g_x[:, :rank],
        g_x[:, rank:],
        g_wdtp,
        g_bias,
        g_alog,
        g_skip,
        grad_wout,
    )


def solution(mesh):
    return jax.shard_map(
        local,
        mesh=mesh,
        in_specs=(
            P(("row", "wide"), None),
            P(("row", "wide")),
            P(),
            P(None, None, None, "wide"),
            P(None, "wide"),
            P("wide"),
            P(),
            P(),
            P(),
            P(),
            P(),
            P(),
            P(None, "wide", None),
            P(("row", "wide"), None),
        ),
        out_specs=(
            P(("row", "wide"), None),
            P(("row", "wide"), None),
            P("wide"),
            P(None, None, None, "wide"),
            P(None, "wide"),
            P("wide"),
            P("wide", None),
            P("wide", None),
            P(None, "wide"),
            P("wide"),
            P(None, "wide"),
            P("wide"),
            P(None, "wide", None),
        ),
        check_vma=False,
    )
```

```python
import functools

import jax
import jax.numpy as jnp
from jax import lax
from jax.experimental import pallas as pl
from jax.experimental.pallas import tpu as pltpu
from jax.sharding import PartitionSpec as P
LOG2E = 1.4426950408889634
EPS = 1e-05
SPAN = 256
TILE = 16
FU, BU = 4, 2

def softplus(v):
    return jnp.maximum(v, 0.0) + jnp.log1p(jnp.exp(-jnp.abs(v)))

def spread(columns, n):
    wide = TILE * n
    pick = lax.broadcasted_iota(jnp.int32, (n, wide), 1) % n == lax.broadcasted_iota(jnp.int32, (n, wide), 0)
    tiled = jnp.dot(columns.astype(jnp.bfloat16), pick.astype(jnp.bfloat16), preferred_element_type=jnp.float32)
    return jnp.where(diagonal(columns.shape[0], n), tiled, 0.0).astype(jnp.bfloat16)

def diagonal(rows, n):
    wide = TILE * n
    return lax.broadcasted_iota(jnp.int32, (rows, wide), 1) // n == lax.broadcasted_iota(jnp.int32, (rows, wide), 0) % TILE

def mm(a, b):
    return jnp.dot(a, b, preferred_element_type=jnp.float32)

def mt(a, b):
    return lax.dot_general(a, b, (((1,), (1,)), ((), ())), preferred_element_type=jnp.float32)

WINDOW = 384
ALIGN = 16

def first_window(bounds, row, m, span, window):
    first, last = bounds[row, m], bounds[row, m + 1]
    base = lax.div(first, ALIGN) * ALIGN
    count = jnp.where(last > first, lax.div(last - base + window - 1, window), 0)
    return first, last, base, count


def inside(at, low, high, window):
    here = at + lax.broadcasted_iota(jnp.int32, (window, 128), 0)
    return jnp.where((here >= low) & (here < high), 1.0, 0.0).astype(jnp.bfloat16)


def grouped_sum(bounds, slots, m, span, window, left_at, right_at, acc, starts):
    lefts, rights, more = [], [], []
    for s in range(slots):
        first, last, base, count = first_window(bounds, s, m, span, window)
        at = pl.multiple_of(jnp.minimum(base, span - window), ALIGN)
        keep = inside(at, first, last, window)
        lefts.append(left_at(s, at, keep))
        rights.append(right_at(s, at, keep))
        more.append((last, base, count))
    total = mm(jnp.concatenate(lefts, 1), jnp.concatenate(rights, 0))
    if starts:
        total = total + jnp.concatenate([start[0] for start in starts], 1)
    acc[...] = total
    for s, (last, base, count) in enumerate(more):

        def one(i, _):
            want = base + i * window
            at = pl.multiple_of(jnp.minimum(want, span - window), ALIGN)
            keep = inside(at, want, last, window)
            acc[...] += mm(left_at(s, at, keep), right_at(s, at, keep))
            return 0

        lax.fori_loop(1, count, one, 0)


def choose(picks, choices, refs, held):
    @pl.when((pl.program_id(0) == 0) & (pl.program_id(1) == 0))
    def _():
        at = 0
        for i, count in enumerate(choices):
            for j in range(count):

                @pl.when(picks[i] == j)
                def _(ref=refs[at + j], i=i):
                    held[i] = ref[...]

            at += count


def grad_in_kernel(bounds, picks, *refs, slots, choices, begun, halves):
    total = sum(choices)
    rows, d, starts = refs[:slots], refs[slots : slots + total], refs[slots + total : -3]
    out, acc, held = refs[-3:]
    parts = len(choices) // slots
    wide, _, unit, bf = rows[0].shape
    span, chan = d[0].shape
    window = min(WINDOW, span)
    choose(picks, choices, d, held)

    def left_at(s, at, keep):
        return jnp.transpose(rows[s].reshape(span, bf)[pl.ds(at, window), :])

    def right_at(s, at, keep):
        tiled = jnp.concatenate([keep] * (chan // 128), 1)
        return jnp.concatenate([held[s * parts + p, pl.ds(at, window), :] * tiled for p in range(parts)], 1)

    grouped_sum(bounds, slots, pl.program_id(1), span, window, left_at, right_at, acc, starts)
    if halves:
        tiles = chan // 128
        for h in range(2):
            for j in range(tiles):
                at = h * chan + j * 128
                out[0, pl.ds(j * 2 + h, bf, stride=2 * tiles), :] = acc[:, at : at + 128]
    else:
        out[0] = acc[...]


def slot_spec(array, index, bf):
    return pl.BlockSpec((array.shape[0], 1, array.shape[2], bf), lambda f, m, b, p: (0, index, 0, f))


def side_spec(array, chan, side):
    return pl.BlockSpec((array.shape[0], chan), lambda f, m, b, p: (0, side))


def feature_block(rows):
    wide, _, unit, width = rows[0][0].shape
    return max(128, min(1024, (1 << 20) // (wide * unit)))


def grad_in(bounds, rows, d, mods, chan, starts=()):
    width = rows[0][0].shape[3]
    bf = feature_block(rows)
    slots, parts = len(d), len(d[0])
    flat = [part for entry in d for part in entry]
    choices = tuple(len(arrays) for arrays, _, _ in flat)
    picks = jnp.stack([jnp.asarray(pick, jnp.int32) for _, pick, _ in flat])
    span = flat[0][0][0].shape[0]
    plain = pl.BlockSpec((1, bf, chan), lambda f, m, b, p: (m, f, 0))
    ins = [slot_spec(array, index, bf) for array, index in rows]
    args = [array for array, _ in rows]
    for arrays, _, side in flat:
        for x in arrays:
            ins.append(side_spec(x, chan, side))
            args.append(x)
    for start in starts:
        ins.append(plain)
        args.append(start)
    if parts == 2:
        out_shape = jax.ShapeDtypeStruct((mods, width * 2 * chan // 128, 128), jnp.float32)
        out_spec = pl.BlockSpec((1, bf * 2 * chan // 128, 128), lambda f, m, b, p: (m, f, 0))
    else:
        out_shape = jax.ShapeDtypeStruct((mods, width, chan), jnp.float32)
        out_spec = plain
    return pl.pallas_call(
        functools.partial(grad_in_kernel, slots=slots, choices=choices, begun=bool(starts), halves=parts == 2),
        grid_spec=pltpu.PrefetchScalarGridSpec(
            num_scalar_prefetch=2,
            grid=(width // bf, mods),
            in_specs=ins,
            out_specs=out_spec,
            scratch_shapes=[pltpu.VMEM((bf, parts * chan), jnp.float32), pltpu.VMEM((len(flat), span, chan), jnp.bfloat16)],
        ),
        out_shape=out_shape,
        compiler_params=pltpu.CompilerParams(vmem_limit_bytes=58 << 20),
    )(bounds, picks, *args)


def grad_out_kernel(bounds, picks, *refs, slots, choices):
    cot, gated, out, held = refs[:slots], refs[slots:-2], refs[-2], refs[-1]
    wide, _, unit, bf = cot[0].shape
    span, chan = gated[0].shape
    window = min(WINDOW, span)
    choose(picks, choices, gated, held)

    def left_at(s, at, keep):
        return jnp.transpose(held[s, pl.ds(at, window), :] * jnp.concatenate([keep] * (chan // 128), 1))

    def right_at(s, at, keep):
        return cot[s].reshape(span, bf)[pl.ds(at, window), :]

    grouped_sum(bounds, slots, pl.program_id(1), span, window, left_at, right_at, out.at[0], ())


def grad_out(bounds, cot, gated, mods, chan):
    width = cot[0][0].shape[3]
    bf = feature_block(cot)
    slots = len(gated)
    choices = tuple(len(arrays) for arrays, _, _ in gated)
    picks = jnp.stack([jnp.asarray(pick, jnp.int32) for _, pick, _ in gated])
    span = gated[0][0][0].shape[0]
    return pl.pallas_call(
        functools.partial(grad_out_kernel, slots=slots, choices=choices),
        grid_spec=pltpu.PrefetchScalarGridSpec(
            num_scalar_prefetch=2,
            grid=(width // bf, mods),
            in_specs=[slot_spec(array, index, bf) for array, index in cot]
            + [side_spec(x, chan, side) for arrays, _, side in gated for x in arrays],
            out_specs=pl.BlockSpec((1, chan, bf), lambda f, m, b, p: (m, 0, f)),
            scratch_shapes=[pltpu.VMEM((slots, span, chan), jnp.bfloat16)],
        ),
        out_shape=jax.ShapeDtypeStruct((mods, chan, width), jnp.float32),
        compiler_params=pltpu.CompilerParams(vmem_limit_bytes=58 << 20),
    )(bounds, picks, *[array for array, _ in cot], *[x for arrays, _, _ in gated for x in arrays])


def fwd_kernel(lr, dtw, dtb, cf, ct, u, alog, skip, gate, dgated, gated, dy, dgate, starts, h_s, dt_s, du_s, y_s, bd_s, hb_s):
    span, chan = u.shape
    n = alog.shape[0]
    @pl.when(pl.program_id(0) == 0)
    def _():
        h_s[...] = jnp.zeros_like(h_s)
    rate = -jnp.exp(alog[...]) * LOG2E
    dt = softplus(mm(lr[...], dtw[...]) + dtb[...])
    uf = u[...].astype(jnp.float32)
    dt_s[...] = dt
    du_s[...] = dt * uf
    starts[0] = h_s[...]
    bd_s[...] = spread(cf[:, n:], n)
    block = FU * TILE
    def reduce(g):
        for k in range(FU):
            t0 = pl.multiple_of(g * block + k * TILE, TILE)
            y_s[pl.ds(t0, TILE), :] = mm(bd_s[pl.ds(t0, TILE), :], hb_s[pl.ds(pl.multiple_of(t0 * n, TILE * n), TILE * n), :])
    def group(g, h):
        c = pltpu.roll(ct[:n, :], span - g * block, 1)
        reduce(jnp.maximum(g - 1, 0))
        for j in range(block):
            t = g * block + j
            e = jnp.exp2(dt_s[pl.ds(t, 1), :] * rate)
            h = e * h + du_s[pl.ds(t, 1), :] * c[:, j:j+1]
            hb_s[pl.ds(pl.multiple_of(t * n, n), n), :] = h.astype(jnp.bfloat16)
        return h
    h_s[...] = lax.fori_loop(0, span // block, group, h_s[...])
    reduce(span // block - 1)
    y = (y_s[...] + skip[...] * uf).astype(jnp.bfloat16).astype(jnp.float32)
    g = gate[...]
    sig = jax.nn.sigmoid(g)
    silu = g * sig
    dg = dgated[...]
    gated[...] = (y * silu).astype(jnp.bfloat16)
    dy[...] = (dg * silu).astype(jnp.bfloat16)
    dgate[...] = (dg * y * sig * (1.0 + g * (1.0 - sig))).astype(jnp.bfloat16)

def scan_forward(lr, dtw, dtb, cf, ct, u, alog, skip, gate, dgated, span=SPAN):
    rows, chan = u.shape
    n = alog.shape[0]
    rank = lr.shape[1]
    steps = rows // span
    full = lambda a: pl.BlockSpec(a.shape, lambda i: (0,) * a.ndim)
    tok = lambda w: pl.BlockSpec((span, w), lambda i: (i, 0))
    return pl.pallas_call(
        fwd_kernel, grid=(steps,),
        in_specs=[tok(rank), full(dtw), full(dtb), tok(2*n), pl.BlockSpec((2*n, span), lambda i: (0, i)), tok(chan), full(alog), full(skip), tok(chan), tok(chan)],
        out_specs=[tok(chan)] * 3 + [pl.BlockSpec((1, n, chan), lambda i: (i, 0, 0))],
        out_shape=[jax.ShapeDtypeStruct((rows, chan), jnp.bfloat16)] * 3 + [jax.ShapeDtypeStruct((steps, n, chan), jnp.float32)],
        scratch_shapes=[pltpu.VMEM((n, chan), jnp.float32)] + [pltpu.VMEM((span, chan), jnp.float32)] * 3 + [pltpu.VMEM((span, TILE * n), jnp.bfloat16), pltpu.VMEM((span * n, chan), jnp.bfloat16)],
        compiler_params=pltpu.CompilerParams(vmem_limit_bytes=32 << 20),
    )(lr, dtw, dtb, cf, ct, u, alog, skip, gate, dgated)

def bwd_kernel(lr, dtw, dtb, cf, ct, u, alog, skip, dy, starts, dpre, dval, dlow, din, dout, galog, gskip, gbias, gdtw, lam_s, dt_s, du_s, dyf_s, hp_s, st_s, th_s, bd_s, hb_s, gb_s):
    span, chan = u.shape
    n = alog.shape[0]
    @pl.when(pl.program_id(0) == 0)
    def _():
        lam_s[...] = jnp.zeros_like(lam_s)
        galog[...] = jnp.zeros_like(galog)
        gskip[...] = jnp.zeros_like(gskip)
        gbias[...] = jnp.zeros_like(gbias)
        gdtw[...] = jnp.zeros_like(gdtw)
    decay = -jnp.exp(alog[...])
    rate = decay * LOG2E
    pre = mm(lr[...], dtw[...]) + dtb[...]
    dt = softplus(pre)
    uf = u[...].astype(jnp.float32)
    dyf = dy[...].astype(jnp.float32)
    dt_s[...] = dt
    du_s[...] = dt * uf
    dyf_s[...] = dyf
    bd_s[...] = spread(cf[:, :n], n)
    mask = diagonal(TILE, n)
    ones = mask.astype(jnp.bfloat16)
    block = FU * TILE
    def reduce_h(g):
        for k in range(FU):
            t0 = pl.multiple_of(g * block + k * TILE, TILE)
            cross = mt(dy[pl.ds(t0, TILE), :], hb_s[pl.ds(pl.multiple_of(t0 * n, TILE * n), TILE * n), :])
            dout[0, pl.ds(g * FU + k, 1), :] = jnp.sum(jnp.where(mask, cross, 0.0), axis=0, keepdims=True)
    def again(g, h):
        c = pltpu.roll(ct[:n, :], span - g * block, 1)
        reduce_h(jnp.maximum(g - 1, 0))
        for j in range(block):
            t = g * block + j
            hp_s[t] = h
            e = jnp.exp2(dt_s[pl.ds(t, 1), :] * rate)
            h = e * h + du_s[pl.ds(t, 1), :] * c[:, j:j+1]
            hb_s[pl.ds(pl.multiple_of(t * n, n), n), :] = h.astype(jnp.bfloat16)
        return h
    lax.fori_loop(0, span // block, again, starts[0])
    reduce_h(span // block - 1)
    back = BU * TILE
    per = span // back
    def reduce_lam(g):
        for k in range(BU - 1, -1, -1):
            t0 = pl.multiple_of(g * back + k * TILE, TILE)
            wide = pl.ds(pl.multiple_of(t0 * n, TILE * n), TILE * n)
            lam16 = hb_s[wide, :]
            st_s[pl.ds(t0, TILE), :] = mm(ones, gb_s[wide, :])
            th_s[pl.ds(t0, TILE), :] = mm(bd_s[pl.ds(t0, TILE), :], lam16)
            cross = mt(du_s[pl.ds(t0, TILE), :].astype(jnp.bfloat16), lam16)
            din[0, pl.ds(g * BU + k, 1), :] = jnp.sum(jnp.where(mask, cross, 0.0), axis=0, keepdims=True)
    def group(q, state):
        carry, gdec = state
        g = per - 1 - q
        c = pltpu.roll(ct[n:, :], span - g * back, 1)
        reduce_lam(jnp.minimum(g + 1, per - 1))
        for j in range(back - 1, -1, -1):
            t = g * back + j
            here = pl.ds(pl.multiple_of(t * n, n), n)
            d = dt_s[pl.ds(t, 1), :]
            lam = carry + dyf_s[pl.ds(t, 1), :] * c[:, j:j+1]
            carry = lam * jnp.exp2(d * rate)
            grow = carry * hp_s[t]
            gdec = gdec + grow * d
            hb_s[here, :] = lam.astype(jnp.bfloat16)
            gb_s[here, :] = (grow * decay).astype(jnp.bfloat16)
        return carry, gdec
    carry, gdec = lax.fori_loop(0, per, group, (lam_s[...], jnp.zeros_like(decay)))
    reduce_lam(0)
    lam_s[...] = carry
    galog[...] += gdec * decay
    gskip[...] += jnp.sum(dyf * uf, axis=0, keepdims=True)
    thru = th_s[...]
    dp = ((st_s[...] + thru * uf) * jax.nn.sigmoid(pre)).astype(jnp.bfloat16)
    dpre[...] = dp
    dval[...] = thru * dt + skip[...] * dyf
    gbias[...] += jnp.sum(dp.astype(jnp.float32), axis=0, keepdims=True)
    dlow[...] = mt(dp, dtw[...])
    gdtw[...] += lax.dot_general(lr[...], dp, (((0,), (0,)), ((), ())), preferred_element_type=jnp.float32)

def scan_backward(lr, dtw, dtb, cf, ct, u, alog, skip, dy, starts, span=SPAN):
    rows, chan = u.shape
    n = alog.shape[0]
    rank = lr.shape[1]
    steps = rows // span
    full = lambda a: pl.BlockSpec(a.shape, lambda i: (0,) * a.ndim)
    tok = lambda w: pl.BlockSpec((span, w), lambda i: (steps - 1 - i, 0))
    ctok = pl.BlockSpec((2*n, span), lambda i: (0, steps - 1 - i))
    ptok = pl.BlockSpec((1, span // TILE, TILE * n), lambda i: (steps - 1 - i, 0, 0))
    f = lambda *s: jax.ShapeDtypeStruct(s, jnp.float32)
    outs = [jax.ShapeDtypeStruct((rows, chan), jnp.bfloat16), f(rows, chan), f(rows, rank), f(steps, span // TILE, TILE * n), f(steps, span // TILE, TILE * n), f(n, chan), f(1, chan), f(1, chan), f(rank, chan)]
    return pl.pallas_call(
        bwd_kernel, grid=(steps,),
        in_specs=[tok(rank), full(dtw), full(dtb), tok(2*n), ctok, tok(chan), full(alog), full(skip), tok(chan), pl.BlockSpec((1, n, chan), lambda i: (steps - 1 - i, 0, 0))],
        out_specs=[tok(chan), tok(chan), tok(rank), ptok, ptok] + [full(o) for o in outs[5:]],
        out_shape=outs,
        scratch_shapes=[pltpu.VMEM((n, chan), jnp.float32)] + [pltpu.VMEM((span, chan), jnp.float32)] * 3 + [pltpu.VMEM((span, n, chan), jnp.float32)] + [pltpu.VMEM((span, chan), jnp.float32)] * 2 + [pltpu.VMEM((span, TILE * n), jnp.bfloat16)] + [pltpu.VMEM((span * n, chan), jnp.bfloat16)] * 2,
        compiler_params=pltpu.CompilerParams(vmem_limit_bytes=32 << 20),
    )(lr, dtw, dtb, cf, ct, u, alog, skip, dy, starts)


def shifted(block, before, back):
    if back == 0:
        return block
    rows = block.shape[0]
    return jnp.concatenate([before[8 - back :], block[: rows - back]], 0)


def masked_sum(x, masks, weights, product):
    total = None
    for m in range(weights[0].shape[0]):
        held = x * masks[:, m : m + 1]
        parts = [product(held, w[m]) for w in weights]
        total = parts if total is None else [t + p for t, p in zip(total, parts)]
    return total


def enter_kernel(rows, masks, w, cw, cb, xp, conv_in, gate_in, pre_act, conv_out, part, tail):
    @pl.when(pl.program_id(0) == 0)
    def _():
        tail[...] = jnp.zeros_like(tail)

    taps = cw.shape[0]
    unit = masks.shape[0] // rows.shape[0]
    x = jnp.concatenate([rows[k, :unit] for k in range(rows.shape[0])], 0)
    ax, az = masked_sum(x, masks[...], (w.at[0], w.at[1]), mm)
    before = tail[...]
    pre = cb[...]
    for k in range(taps):
        pre = pre + cw[k : k + 1] * shifted(ax, before, taps - 1 - k)
    tail[...] = ax[-8:]
    out = (pre * jax.nn.sigmoid(pre)).astype(jnp.bfloat16)
    conv_in[...] = ax
    gate_in[...] = az
    pre_act[...] = pre
    conv_out[...] = out
    part[...] = mm(out, xp[...])


def whole_spec(a):
    return pl.BlockSpec(a.shape, lambda i: (0,) * len(a.shape))


def enter(rows, masks, w, cw, cb, xp, block):
    wide, padded, width = rows.shape
    span = masks.shape[0]
    chan, small = xp.shape
    tok = lambda w: pl.BlockSpec((block, w), lambda i: (i, 0))
    f = lambda w, t=jnp.float32: jax.ShapeDtypeStruct((span, w), t)
    return pl.pallas_call(
        enter_kernel,
        grid=(span // block,),
        in_specs=[pl.BlockSpec((block * wide // span, padded, width), lambda i: (i, 0, 0)), tok(masks.shape[1])]
        + [whole_spec(a) for a in (w, cw, cb, xp)],
        out_specs=[tok(chan)] * 4 + [tok(small)],
        out_shape=[f(chan), f(chan), f(chan), f(chan, jnp.bfloat16), f(small)],
        scratch_shapes=[pltpu.VMEM((8, chan), jnp.float32)],
        compiler_params=pltpu.CompilerParams(vmem_limit_bytes=56 << 20),
    )(rows, masks, w, cw, cb, xp)


def apply_kernel(masks, *refs, turned):
    *inputs, w, out = refs
    total = None
    for k, x in enumerate(inputs):
        (part,) = masked_sum(x[...], masks[...], (w.at[k],), mt if turned else mm)
        total = part if total is None else total + part
    out[...] = total.astype(out.dtype)


def apply(masks, inputs, w, turned, dtype, block):
    span = masks.shape[0]
    width = w.shape[2 if turned else 3]
    tok = lambda c: pl.BlockSpec((block, c), lambda i: (i, 0))
    return pl.pallas_call(
        functools.partial(apply_kernel, turned=turned),
        grid=(span // block,),
        in_specs=[tok(masks.shape[1])] + [tok(x.shape[1]) for x in inputs] + [whole_spec(w)],
        out_specs=tok(width),
        out_shape=jax.ShapeDtypeStruct((span, width), dtype),
        compiler_params=pltpu.CompilerParams(vmem_limit_bytes=56 << 20),
    )(masks, *inputs, w)


def leave_kernel(dval, dsmall, xp, pre_act, conv_in, prev_in, conv_out, cw, d_conv_in, grad_taps, grad_bias, grad_x, head):
    i = pl.program_id(0)
    steps = pl.num_programs(0)

    @pl.when(i == 0)
    def _():
        head[...] = jnp.zeros_like(head)
        grad_taps[...] = jnp.zeros_like(grad_taps)
        grad_bias[...] = jnp.zeros_like(grad_bias)
        grad_x[...] = jnp.zeros_like(grad_x)

    taps = cw.shape[0]
    d_out = (dval[...] + mt(dsmall[...], xp[...])).astype(jnp.bfloat16).astype(jnp.float32)
    pre = pre_act[...]
    sig = jax.nn.sigmoid(pre)
    d_pre = d_out * sig * (1.0 + pre * (1.0 - sig))
    before = jnp.where(i == steps - 1, 0.0, prev_in[...])
    held = conv_in[...]
    rows = held.shape[0]
    after = head[...]
    total = None
    for k in range(taps):
        back = taps - 1 - k
        grad_taps[k : k + 1] += jnp.sum(d_pre * shifted(held, before, back), axis=0, keepdims=True)
        moved = d_pre if back == 0 else jnp.concatenate([d_pre[back:], after[:back]], 0)
        term = cw[k : k + 1] * moved
        total = term if total is None else total + term
    head[...] = d_pre[:8]
    d_conv_in[...] = total.astype(jnp.bfloat16)
    grad_bias[...] += jnp.sum(d_pre, axis=0, keepdims=True)
    grad_x[...] += lax.dot_general(conv_out[...], dsmall[...], (((0,), (0,)), ((), ())), preferred_element_type=jnp.float32)


def leave(dval, dsmall, xp, pre_act, conv_in, conv_out, cw, block):
    span, chan = pre_act.shape
    steps = span // block
    taps, small = cw.shape[0], xp.shape[1]
    tok = lambda w: pl.BlockSpec((block, w), lambda i: (steps - 1 - i, 0))
    prev = pl.BlockSpec((8, chan), lambda i: (jnp.maximum((steps - 1 - i) * (block // 8) - 1, 0), 0))
    f = lambda *s: jax.ShapeDtypeStruct(s, jnp.float32)
    outs = [jax.ShapeDtypeStruct((span, chan), jnp.bfloat16), f(taps, chan), f(1, chan), f(chan, small)]
    return pl.pallas_call(
        leave_kernel,
        grid=(steps,),
        in_specs=[tok(chan), tok(small), whole_spec(xp), tok(chan), tok(chan), prev, tok(chan), whole_spec(cw)],
        out_specs=[tok(chan)] + [whole_spec(o) for o in outs[1:]],
        out_shape=outs,
        scratch_shapes=[pltpu.VMEM((8, chan), jnp.float32)],
        compiler_params=pltpu.CompilerParams(vmem_limit_bytes=56 << 20),
    )(dval, dsmall, xp, pre_act, conv_in, conv_in, conv_out, cw)


def sort_kernel(start, rank, *refs, pieces):
    inputs, out = refs[:-1], refs[-1]
    rows = out.shape[0]
    span = rank.shape[1]
    first = start[0] + pl.program_id(0) * rows
    here = lax.broadcasted_iota(jnp.int32, (rows, span), 0) + first
    choose = jnp.where(rank[...] == here, 1.0, 0.0).astype(jnp.bfloat16)
    at = 0
    for k in range(0, len(inputs), pieces):
        group = inputs[k : k + pieces]
        x = group[0][...] if pieces == 1 else jnp.concatenate([g[: span // pieces] for g in group], 0)
        out[:, at : at + x.shape[1]] = mm(choose, x).astype(out.dtype)
        at += x.shape[1]


def sort_rows(start, rank, inputs, rows, block, pieces=1):
    span = rank.shape[1]
    width = sum(x.shape[1] for x in inputs) // pieces
    return pl.pallas_call(
        functools.partial(sort_kernel, pieces=pieces),
        grid_spec=pltpu.PrefetchScalarGridSpec(
            num_scalar_prefetch=1,
            grid=(rows // block,),
            in_specs=[pl.BlockSpec((1, span), lambda i, s: (0, 0))]
            + [pl.BlockSpec(x.shape, lambda i, s: (0, 0)) for x in inputs],
            out_specs=pl.BlockSpec((block, width), lambda i, s: (i, 0)),
        ),
        out_shape=jax.ShapeDtypeStruct((rows, width), inputs[0].dtype),
        compiler_params=pltpu.CompilerParams(vmem_limit_bytes=40 << 20),
    )(start, rank, *inputs)


def blocks_kernel(place, masks, *refs, pairs):
    blocks, w, out = refs[:-2], refs[-2], refs[-1]
    unit = blocks[0].shape[0]
    core, chip = place[0] % 2, place[0] // 2
    for k in range(pairs):
        here = pl.multiple_of((chip ^ k) * 2 * unit, 2 * unit)
        low = pl.ds(pl.multiple_of(here + core * unit, unit), unit)
        high = pl.ds(pl.multiple_of(here + (1 - core) * unit, unit), unit)
        x = jnp.concatenate([blocks[2 * k][...], blocks[2 * k + 1][...]], 0)
        marks = jnp.concatenate([masks[low, :], masks[high, :]], 0)
        (total,) = masked_sum(x, marks, (w,), mt)
        out[low, :] = total[:unit]
        out[high, :] = total[unit:]


def apply_blocks(place, masks, blocks, w):
    span, chan = masks.shape[0], w.shape[1]
    return pl.pallas_call(
        functools.partial(blocks_kernel, pairs=len(blocks) // 2),
        grid_spec=pltpu.PrefetchScalarGridSpec(
            num_scalar_prefetch=1,
            grid=(1,),
            in_specs=[pl.BlockSpec(a.shape, lambda i, s, n=a.ndim: (0,) * n) for a in (masks, *blocks, w)],
            out_specs=pl.BlockSpec((span, chan), lambda i, s: (0, 0)),
        ),
        out_shape=jax.ShapeDtypeStruct((span, chan), jnp.float32),
        compiler_params=pltpu.CompilerParams(vmem_limit_bytes=40 << 20),
    )(place, masks, *blocks, w)


def contract(left, right, left_dim, right_dim):
    return lax.dot_general(
        left, right, (((left_dim,), (right_dim,)), ((), ())), preferred_element_type=jnp.float32
    )


def own(array, dim, size):
    return lax.dynamic_slice_in_dim(array, lax.axis_index("wide") * size, size, dim)


def pick(array, index, dim=0):
    return lax.dynamic_index_in_dim(array, index, dim, False)


def cross(array, k):
    return lax.ppermute(array, "wide", [(i, i ^ k) for i in range(lax.axis_size("wide"))])


def begin_gather(shard):
    if lax.axis_size("wide") != 8:
        return (shard,)
    return shard, cross(shard, 2), cross(shard, 4), cross(shard, 1)


def end_gather(begun, work):
    if lax.axis_size("wide") != 8:
        whole = lax.all_gather(begun[0], "wide", axis=0)
        return [whole[k] for k in range(whole.shape[0])], work()
    shard, by_x, by_y, pair = begun
    half = shard.shape[0] // 2
    far = (cross(by_y[:half], 2), cross(by_x[half:], 4))
    pair_x, pair_y = cross(by_x, 1), cross(by_y, 1)
    beside, *far = lax.optimization_barrier((work(),) + far)
    far = jnp.concatenate(far, 0)
    return [shard, pair, by_x, pair_x, by_y, pair_y, far, cross(far, 1)], beside


def assemble(blocks):
    if lax.axis_size("wide") != 8:
        return jnp.stack(blocks)
    here = lax.axis_index("wide")
    whole = jnp.zeros((8,) + blocks[0].shape, blocks[0].dtype)
    for k, block in enumerate(blocks):
        whole = lax.dynamic_update_index_in_dim(whole, block, here ^ k, 0)
    return whole


def sum_wide(part, held, work, ordered=True):
    if lax.axis_size("wide") != 8:
        return lax.psum(part, "wide"), work(held)
    half = part.shape[0] // 2
    core = lax.axis_index("wide") % 2
    mine = lax.dynamic_slice_in_dim(part, core * half, half, 0)
    other = lax.dynamic_slice_in_dim(part, (1 - core) * half, half, 0)
    mine = mine + cross(other, 1)
    if ordered:
        mine, held = lax.optimization_barrier((mine, held))
    sent = mine.astype(jnp.bfloat16)
    beside, *came = lax.optimization_barrier((work(held),) + tuple(cross(sent, k) for k in (2, 4, 6)))
    total = mine
    for block in came:
        total = total + block.astype(jnp.float32)
    other = cross(total, 1)
    return jnp.where(core == 0, jnp.concatenate([total, other], 0), jnp.concatenate([other, total], 0)), beside


def scatter_wide(part):
    return lax.psum_scatter(part, "wide", scatter_dimension=0, tiled=True).astype(jnp.float32)


def after(value, *first):
    return lax.optimization_barrier((value,) + first)[0]


def hop(rising, falling):
    return (
        lax.ppermute(rising, "row", [(0, 1), (1, 2), (2, 3)]),
        lax.ppermute(falling, "row", [(1, 0), (2, 1), (3, 2)]),
    )


def near_slot(hops, side):
    here = lax.axis_index("row")
    return (hops[0][0], hops[0][1]), jnp.where(here == 0, 1, 0), side


def middle_slot(hops, side):
    return (hops[1][0], hops[1][1]), jnp.where(lax.axis_index("row") < 2, 1, 0), side


def last_slot(hops, side):
    here = lax.axis_index("row")
    return (hops[0][1], hops[2][0], hops[2][1]), jnp.where(here == 3, 1, jnp.where(here == 0, 2, 0)), side


def only(array, side):
    return (array,), 0, side


def sum_row(part):
    if lax.axis_size("row") != 4:
        return lax.psum(part, "row")
    for k in (1, 2):
        part = part + lax.ppermute(part, "row", [(i, i ^ k) for i in range(4)])
    return part


def sum_row_low(part, beside):
    if lax.axis_size("row") != 4:
        return lax.psum(part.astype(jnp.bfloat16), "row").astype(jnp.float32), beside
    for k in (1, 2):
        sent = lax.ppermute(part.astype(jnp.bfloat16), "row", [(i, i ^ k) for i in range(4)])
        if k == 1:
            sent, beside = lax.optimization_barrier((sent, beside))
        part = part + sent.astype(jnp.float32)
    return part, beside


def share_wide(part):
    count = lax.axis_size("wide")
    if count != 8:
        return lax.psum_scatter(part, "wide", scatter_dimension=0, tiled=True)
    for k in (1, 2, 4):
        part = part + cross(part, k)
    return own(part, 0, part.shape[0] // count)


def row_order():
    count = lax.axis_size("row")
    here = lax.axis_index("row")
    if count != 4:
        return [lax.rem(here + s, count) for s in range(count)]
    near = jnp.where(here == 0, 1, here - 1)
    last = jnp.where(here == 3, 0, jnp.where(here == 0, 3, here + 1))
    return [here, near, lax.rem(here + 2, 4), last]


def others(array, order):
    return jnp.stack([pick(array, q) for q in order[1:]], 0)


def gather_ordered(block, order):
    whole = lax.all_gather(block, "row", axis=0)
    return [block] + [pick(whole, q) for q in order[1:]]


def sorted_places(ids, mods):
    one = (ids[:, None] == jnp.arange(mods, dtype=ids.dtype)[None]).astype(jnp.int32)
    before = jnp.cumsum(one, 0)
    total = before[-1]
    first = jnp.cumsum(total) - total
    return jnp.sum(one * (before - 1 + first[None]), 1)[None]


def group_bounds(ids, mods):
    count = jnp.sum((ids[:, None] == jnp.arange(mods, dtype=ids.dtype)).astype(jnp.int32), 0)
    return jnp.concatenate([jnp.zeros((1,), jnp.int32), jnp.cumsum(count)], 0)


def local(
    hidden,
    modality,
    norm_gain,
    in_proj,
    conv_weight,
    conv_bias,
    x_proj_dt,
    x_proj_bc,
    dt_proj,
    dt_bias,
    a_log,
    skip_weight,
    out_proj,
    cotangent,
):
    shard_rows, width = hidden.shape
    mods = in_proj.shape[0]
    chan = in_proj.shape[3]
    taps = conv_weight.shape[0]
    n = a_log.shape[0]
    rank = dt_proj.shape[0]
    row_count = lax.axis_size("row")
    residual = hidden.astype(jnp.float32)
    inv_rms = lax.rsqrt(jnp.mean(residual * residual, axis=-1, keepdims=True) + EPS)
    gain_vec = norm_gain.astype(jnp.float32)
    normed = (residual * inv_rms * gain_vec).astype(jnp.bfloat16)
    lanes = jnp.pad(modality.astype(jnp.bfloat16)[None], ((0, 15), (0, width - shard_rows)))
    conv_taps = conv_weight.astype(jnp.float32)
    w_out = out_proj[None]

    def small_slices():
        x_proj = jnp.concatenate([own(x_proj_dt, 0, chan), own(x_proj_bc, 0, chan)], 1)
        return x_proj, own(dt_proj, 1, chan), own(dt_bias, 0, chan)[None], own(a_log, 1, chan), own(skip_weight, 0, chan)[None]

    begun = begin_gather(jnp.concatenate([normed, lanes], 0))
    begun, w_in = lax.optimization_barrier((begun, jnp.transpose(in_proj, (2, 0, 1, 3))))
    row_blocks, (x_proj, dtw, dtb, alog, skip) = end_gather(begun, small_slices)
    rows = assemble(row_blocks)
    ids = rows[:, shard_rows, :shard_rows].astype(jnp.int32).reshape(-1)
    masks = (ids[:, None] == jnp.arange(128, dtype=ids.dtype)[None]).astype(jnp.bfloat16)
    span_rows = ids.shape[0]
    block = min(256, span_rows)
    order = row_order()
    slot = jnp.arange(row_count, dtype=jnp.int32)[:, None] == lax.axis_index("row")
    whole = jnp.zeros((1,), jnp.int32)
    chunk = lax.axis_index("wide").astype(jnp.int32)[None] * shard_rows
    places = sorted_places(ids, mods)
    pieces = len(row_blocks)
    here = lax.axis_index("wide").astype(jnp.int32)
    if pieces == 8:
        swapped = places.reshape(pieces, shard_rows)
        block_places = jnp.concatenate([pick(swapped, here ^ k)[None] for k in range(pieces)], 1)
    else:
        block_places = places
    rows_chunk = sort_rows(chunk, block_places, row_blocks, shard_rows, shard_rows, pieces)
    rows, rows_chunk = lax.optimization_barrier((rows, rows_chunk))
    rows_near = lax.all_gather(rows_chunk, "row", axis=0)
    cot_begun = begin_gather(after(cotangent, rows_chunk))
    conv_in, gate_in, pre_act, conv_out, part = enter(
        rows, masks, w_in, conv_taps, conv_bias.astype(jnp.float32)[None], x_proj, block
    )
    part, cot_begun = lax.optimization_barrier((part, cot_begun))

    cot_blocks, _ = end_gather(cot_begun, lambda: ())

    def first_work(cot_blocks):
        cot_chunk = sort_rows(chunk, block_places, cot_blocks, shard_rows, shard_rows, pieces)
        if pieces == 8:
            d_gated = apply_blocks(here[None], masks, cot_blocks, out_proj)
        else:
            d_gated = apply(masks, (jnp.concatenate(cot_blocks, 0),), w_out, True, jnp.float32, block)
        return cot_chunk, d_gated

    small, (cot_chunk, d_gated) = sum_wide(part, cot_blocks, first_work, False)
    cot_near = lax.all_gather(cot_chunk, "row", axis=0)
    low_rank = small[:, :rank].astype(jnp.bfloat16)
    coefs = small[:, rank:]
    gated, d_y, d_gate_in, starts = scan_forward(
        low_rank, dtw, dtb, coefs, coefs.T, conv_out, alog, skip, gate_in, d_gated
    )
    line = row_count == 4
    gates = sort_rows(whole, places, (gated, d_gate_in), span_rows, block)
    bounds = sum_row(jnp.where(slot, group_bounds(after(ids, part), mods)[None], 0))
    bounds = jnp.stack([pick(bounds, q) for q in order], 0)
    d_y, gates, bounds, rows_near = lax.optimization_barrier((d_y, gates, bounds, rows_near))
    rows_far = lax.all_gather(others(rows_near, order), "wide", axis=0)
    gate_hops = [hop(gates, gates)] if line else []
    d_pre_step, d_value, d_low_part, d_in, d_out, grad_alog, grad_skip, grad_bias, grad_wdtp = scan_backward(
        low_rank, dtw, dtb, coefs, coefs.T, conv_out, alog, skip, d_y, starts
    )
    d_part = jnp.concatenate([d_low_part, d_in.reshape(span_rows, n), d_out.reshape(span_rows, n)], 1)
    d_part, cot_near, gate_hops = lax.optimization_barrier((d_part, cot_near, gate_hops))
    cot_far = lax.all_gather(others(cot_near, order), "wide", axis=0)

    def third_work(gated):
        part = apply(masks, (gated,), w_out, False, jnp.bfloat16, block)
        return part

    d_small, projected = sum_wide(d_part, gated, third_work)
    if line:
        gate_hops.append(hop(*gate_hops[0]))
    d_small = d_small.astype(jnp.bfloat16)
    d_conv_in, grad_taps, grad_cbias, grad_x = leave(
        d_value, d_small, x_proj, pre_act, conv_in, conv_out, conv_taps, block
    )
    conv_sorted = sort_rows(whole, places, (d_conv_in,), span_rows, block)
    d_conv_in, conv_sorted = lax.optimization_barrier((d_conv_in, conv_sorted))
    conv_hops = [hop(conv_sorted, conv_sorted)] if line else []
    normed_part = apply(masks, (d_conv_in, d_gate_in), w_in, True, jnp.bfloat16, block)
    normed_part, rows_far = lax.optimization_barrier((normed_part, rows_far))
    if line:
        normed_part, gate_hops[1] = lax.optimization_barrier((normed_part, gate_hops[1]))
        gate_hops.append(hop(*gate_hops[1]))
    rows_sorted = sort_rows(whole, block_places, [after(x, normed_part) for x in row_blocks], span_rows, block, pieces)
    cot_sorted = sort_rows(whole, block_places, [after(x, normed_part) for x in cot_blocks], span_rows, block, pieces)
    if line:
        rows_sorted, cot_sorted, conv_hops[0] = lax.optimization_barrier((rows_sorted, cot_sorted, conv_hops[0]))
        conv_hops.append(hop(*conv_hops[0]))
        gates_all = lambda side: [only(gates, side), near_slot(gate_hops, side), middle_slot(gate_hops, side)]
    else:
        gates_rows = gather_ordered(gates, order)
        gates_all = lambda side: [only(g, side) for g in gates_rows]
        conv_all = [only(d, 0) for d in gather_ordered(conv_sorted, order)]
    apart = lambda a: a.reshape(span_rows // shard_rows, 1, shard_rows, width)
    far = range(row_count - 1)
    rows_slots = [(apart(rows_sorted), 0)] + [(rows_far, s) for s in far]
    cot_slots = [(apart(cot_sorted), 0)] + [(cot_far, s) for s in far]
    most = len(far)
    z_most = grad_in(bounds[:-1], rows_slots[:-1], [(g,) for g in gates_all(1)[:most]], mods, chan)
    d_normed = scatter_wide(normed_part)
    weighted = gain_vec * d_normed
    grad_hidden = (
        cotangent.astype(jnp.float32)
        + inv_rms * weighted
        - residual * inv_rms * inv_rms * inv_rms * jnp.mean(weighted * residual, axis=-1, keepdims=True)
    )
    g_gain = sum_row(share_wide(jnp.sum(d_normed * residual * inv_rms, 0)))

    small_grads = (grad_taps, grad_cbias[0], grad_x, grad_wdtp, grad_bias[0], grad_alog, grad_skip[0])
    flat = after(jnp.concatenate([g.reshape(-1) for g in small_grads]).reshape(-1, 128), z_most)
    z_most, cot_far = lax.optimization_barrier((z_most, cot_far))
    cot_slots = [(apart(cot_sorted), 0)] + [(cot_far, s) for s in far]
    if line:
        z_most, gate_hops[2], conv_hops[1] = lax.optimization_barrier((z_most, gate_hops[2], conv_hops[1]))
        conv_hops.append(hop(*conv_hops[1]))
        conv_all = [only(conv_sorted, 0), near_slot(conv_hops, 0), middle_slot(conv_hops, 0)]
        gates_all = [[*gates_all(side), last_slot(gate_hops, side)] for side in (0, 1)]
    else:
        gates_all = [gates_all(0), gates_all(1)]
    x_most = grad_in(bounds[:-1], rows_slots[:-1], [(d,) for d in conv_all[:most]], mods, chan)
    output = (residual + scatter_wide(after(projected, normed_part))).astype(jnp.bfloat16)
    flat, x_most = sum_row_low(flat, x_most)
    grad_wout = grad_out(bounds, cot_slots, gates_all[0], mods, chan)
    if line:
        x_most, grad_wout, conv_hops[2] = lax.optimization_barrier((x_most, grad_wout, conv_hops[2]))
        conv_all.append(last_slot(conv_hops, 0))
    grad_win = grad_in(bounds[-1:], rows_slots[-1:], [(conv_all[-1], gates_all[1][-1])], mods, chan, (x_most, z_most))
    grad_win = grad_win.reshape(mods, width, chan // 128, 2, 128).transpose(0, 1, 3, 2, 4).reshape(mods, width, 2, chan)
    flat = flat.reshape(-1)
    summed, at = [], 0
    for g in small_grads:
        summed.append(flat[at : at + g.size].reshape(g.shape))
        at += g.size
    g_taps, g_cbias, g_x, g_wdtp, g_bias, g_alog, g_skip = summed
    return (
        output,
        grad_hidden,
        g_gain,
        grad_win,
        g_taps,
        g_cbias,
        g_x[:, :rank],
        g_x[:, rank:],
        g_wdtp,
        g_bias,
        g_alog,
        g_skip,
        grad_wout,
    )


def solution(mesh):
    return jax.shard_map(
        local,
        mesh=mesh,
        in_specs=(
            P(("row", "wide"), None),
            P(("row", "wide")),
            P(),
            P(None, None, None, "wide"),
            P(None, "wide"),
            P("wide"),
            P(),
            P(),
            P(),
            P(),
            P(),
            P(),
            P(None, "wide", None),
            P(("row", "wide"), None),
        ),
        out_specs=(
            P(("row", "wide"), None),
            P(("row", "wide"), None),
            P("wide"),
            P(None, None, None, "wide"),
            P(None, "wide"),
            P("wide"),
            P("wide", None),
            P("wide", None),
            P(None, "wide"),
            P("wide"),
            P(None, "wide"),
            P("wide"),
            P(None, "wide", None),
        ),
        check_vma=False,
    )
```

```python
import functools

import jax
import jax.numpy as jnp
from jax import lax
from jax.experimental import pallas as pl
from jax.experimental.pallas import tpu as pltpu
from jax.sharding import PartitionSpec as P
LOG2E = 1.4426950408889634
EPS = 1e-05
SPAN = 256
TILE = 16
FU, BU = 4, 2

def softplus(v):
    return jnp.maximum(v, 0.0) + jnp.log1p(jnp.exp(-jnp.abs(v)))

def spread(columns, n):
    wide = TILE * n
    pick = lax.broadcasted_iota(jnp.int32, (n, wide), 1) % n == lax.broadcasted_iota(jnp.int32, (n, wide), 0)
    tiled = jnp.dot(columns.astype(jnp.bfloat16), pick.astype(jnp.bfloat16), preferred_element_type=jnp.float32)
    return jnp.where(diagonal(columns.shape[0], n), tiled, 0.0).astype(jnp.bfloat16)

def diagonal(rows, n):
    wide = TILE * n
    return lax.broadcasted_iota(jnp.int32, (rows, wide), 1) // n == lax.broadcasted_iota(jnp.int32, (rows, wide), 0) % TILE

def mm(a, b):
    return jnp.dot(a, b, preferred_element_type=jnp.float32)

def mt(a, b):
    return lax.dot_general(a, b, (((1,), (1,)), ((), ())), preferred_element_type=jnp.float32)

WINDOW = 384
ALIGN = 16

def first_window(bounds, row, m, span, window):
    first, last = bounds[row, m], bounds[row, m + 1]
    base = lax.div(first, ALIGN) * ALIGN
    count = jnp.where(last > first, lax.div(last - base + window - 1, window), 0)
    return first, last, base, count


def inside(at, low, high, window):
    here = at + lax.broadcasted_iota(jnp.int32, (window, 128), 0)
    return jnp.where((here >= low) & (here < high), 1.0, 0.0).astype(jnp.bfloat16)


def grouped_sum(bounds, slots, m, span, window, left_at, right_at, acc, starts):
    lefts, rights, more = [], [], []
    for s in range(slots):
        first, last, base, count = first_window(bounds, s, m, span, window)
        at = pl.multiple_of(jnp.minimum(base, span - window), ALIGN)
        keep = inside(at, first, last, window)
        lefts.append(left_at(s, at, keep))
        rights.append(right_at(s, at, keep))
        more.append((last, base, count))
    total = mm(jnp.concatenate(lefts, 1), jnp.concatenate(rights, 0))
    if starts:
        total = total + jnp.concatenate([start[0] for start in starts], 1)
    acc[...] = total
    for s, (last, base, count) in enumerate(more):

        def one(i, _):
            want = base + i * window
            at = pl.multiple_of(jnp.minimum(want, span - window), ALIGN)
            keep = inside(at, want, last, window)
            acc[...] += mm(left_at(s, at, keep), right_at(s, at, keep))
            return 0

        lax.fori_loop(1, count, one, 0)


def choose(picks, choices, refs, held):
    @pl.when((pl.program_id(0) == 0) & (pl.program_id(1) == 0))
    def _():
        at = 0
        for i, count in enumerate(choices):
            for j in range(count):

                @pl.when(picks[i] == j)
                def _(ref=refs[at + j], i=i):
                    held[i] = ref[...]

            at += count


def grad_in_kernel(bounds, picks, *refs, slots, choices, begun, halves):
    total = sum(choices)
    rows, d, starts = refs[:slots], refs[slots : slots + total], refs[slots + total : -3]
    out, acc, held = refs[-3:]
    parts = len(choices) // slots
    wide, _, unit, bf = rows[0].shape
    span, chan = d[0].shape
    window = min(WINDOW, span)
    choose(picks, choices, d, held)

    def left_at(s, at, keep):
        return jnp.transpose(rows[s].reshape(span, bf)[pl.ds(at, window), :])

    def right_at(s, at, keep):
        tiled = jnp.concatenate([keep] * (chan // 128), 1)
        return jnp.concatenate([held[s * parts + p, pl.ds(at, window), :] * tiled for p in range(parts)], 1)

    grouped_sum(bounds, slots, pl.program_id(1), span, window, left_at, right_at, acc, starts)
    if halves:
        tiles = chan // 128
        for h in range(2):
            for j in range(tiles):
                at = h * chan + j * 128
                out[0, pl.ds(j * 2 + h, bf, stride=2 * tiles), :] = acc[:, at : at + 128]
    else:
        out[0] = acc[...]


def slot_spec(array, index, bf):
    return pl.BlockSpec((array.shape[0], 1, array.shape[2], bf), lambda f, m, b, p: (0, index, 0, f))


def side_spec(array, chan, side):
    return pl.BlockSpec((array.shape[0], chan), lambda f, m, b, p: (0, side))


def feature_block(rows):
    wide, _, unit, width = rows[0][0].shape
    return max(128, min(1024, (1 << 20) // (wide * unit)))


def grad_in(bounds, rows, d, mods, chan, starts=()):
    width = rows[0][0].shape[3]
    bf = feature_block(rows)
    slots, parts = len(d), len(d[0])
    flat = [part for entry in d for part in entry]
    choices = tuple(len(arrays) for arrays, _, _ in flat)
    picks = jnp.stack([jnp.asarray(pick, jnp.int32) for _, pick, _ in flat])
    span = flat[0][0][0].shape[0]
    plain = pl.BlockSpec((1, bf, chan), lambda f, m, b, p: (m, f, 0))
    ins = [slot_spec(array, index, bf) for array, index in rows]
    args = [array for array, _ in rows]
    for arrays, _, side in flat:
        for x in arrays:
            ins.append(side_spec(x, chan, side))
            args.append(x)
    for start in starts:
        ins.append(plain)
        args.append(start)
    if parts == 2:
        out_shape = jax.ShapeDtypeStruct((mods, width * 2 * chan // 128, 128), jnp.float32)
        out_spec = pl.BlockSpec((1, bf * 2 * chan // 128, 128), lambda f, m, b, p: (m, f, 0))
    else:
        out_shape = jax.ShapeDtypeStruct((mods, width, chan), jnp.float32)
        out_spec = plain
    return pl.pallas_call(
        functools.partial(grad_in_kernel, slots=slots, choices=choices, begun=bool(starts), halves=parts == 2),
        grid_spec=pltpu.PrefetchScalarGridSpec(
            num_scalar_prefetch=2,
            grid=(width // bf, mods),
            in_specs=ins,
            out_specs=out_spec,
            scratch_shapes=[pltpu.VMEM((bf, parts * chan), jnp.float32), pltpu.VMEM((len(flat), span, chan), jnp.bfloat16)],
        ),
        out_shape=out_shape,
        compiler_params=pltpu.CompilerParams(vmem_limit_bytes=58 << 20),
    )(bounds, picks, *args)


def grad_out_kernel(bounds, picks, *refs, slots, choices):
    cot, gated, out, held = refs[:slots], refs[slots:-2], refs[-2], refs[-1]
    wide, _, unit, bf = cot[0].shape
    span, chan = gated[0].shape
    window = min(WINDOW, span)
    choose(picks, choices, gated, held)

    def left_at(s, at, keep):
        return jnp.transpose(held[s, pl.ds(at, window), :] * jnp.concatenate([keep] * (chan // 128), 1))

    def right_at(s, at, keep):
        return cot[s].reshape(span, bf)[pl.ds(at, window), :]

    grouped_sum(bounds, slots, pl.program_id(1), span, window, left_at, right_at, out.at[0], ())


def grad_out(bounds, cot, gated, mods, chan):
    width = cot[0][0].shape[3]
    bf = feature_block(cot)
    slots = len(gated)
    choices = tuple(len(arrays) for arrays, _, _ in gated)
    picks = jnp.stack([jnp.asarray(pick, jnp.int32) for _, pick, _ in gated])
    span = gated[0][0][0].shape[0]
    return pl.pallas_call(
        functools.partial(grad_out_kernel, slots=slots, choices=choices),
        grid_spec=pltpu.PrefetchScalarGridSpec(
            num_scalar_prefetch=2,
            grid=(width // bf, mods),
            in_specs=[slot_spec(array, index, bf) for array, index in cot]
            + [side_spec(x, chan, side) for arrays, _, side in gated for x in arrays],
            out_specs=pl.BlockSpec((1, chan, bf), lambda f, m, b, p: (m, 0, f)),
            scratch_shapes=[pltpu.VMEM((slots, span, chan), jnp.bfloat16)],
        ),
        out_shape=jax.ShapeDtypeStruct((mods, chan, width), jnp.float32),
        compiler_params=pltpu.CompilerParams(vmem_limit_bytes=58 << 20),
    )(bounds, picks, *[array for array, _ in cot], *[x for arrays, _, _ in gated for x in arrays])


def fwd_kernel(lr, dtw, dtb, cf, ct, u, alog, skip, gate, dgated, gated, dy, dgate, starts, h_s, dt_s, du_s, y_s, bd_s, hb_s):
    span, chan = u.shape
    n = alog.shape[0]
    @pl.when(pl.program_id(0) == 0)
    def _():
        h_s[...] = jnp.zeros_like(h_s)
    rate = -jnp.exp(alog[...]) * LOG2E
    dt = softplus(mm(lr[...], dtw[...]) + dtb[...])
    uf = u[...].astype(jnp.float32)
    dt_s[...] = dt
    du_s[...] = dt * uf
    starts[0] = h_s[...]
    bd_s[...] = spread(cf[:, n:], n)
    block = FU * TILE
    def reduce(g):
        for k in range(FU):
            t0 = pl.multiple_of(g * block + k * TILE, TILE)
            y_s[pl.ds(t0, TILE), :] = mm(bd_s[pl.ds(t0, TILE), :], hb_s[pl.ds(pl.multiple_of(t0 * n, TILE * n), TILE * n), :])
    def group(g, h):
        c = pltpu.roll(ct[:n, :], span - g * block, 1)
        reduce(jnp.maximum(g - 1, 0))
        for j in range(block):
            t = g * block + j
            e = jnp.exp2(dt_s[pl.ds(t, 1), :] * rate)
            h = e * h + du_s[pl.ds(t, 1), :] * c[:, j:j+1]
            hb_s[pl.ds(pl.multiple_of(t * n, n), n), :] = h.astype(jnp.bfloat16)
        return h
    h_s[...] = lax.fori_loop(0, span // block, group, h_s[...])
    reduce(span // block - 1)
    y = (y_s[...] + skip[...] * uf).astype(jnp.bfloat16).astype(jnp.float32)
    g = gate[...]
    sig = jax.nn.sigmoid(g)
    silu = g * sig
    dg = dgated[...]
    gated[...] = (y * silu).astype(jnp.bfloat16)
    dy[...] = (dg * silu).astype(jnp.bfloat16)
    dgate[...] = (dg * y * sig * (1.0 + g * (1.0 - sig))).astype(jnp.bfloat16)

def scan_forward(lr, dtw, dtb, cf, ct, u, alog, skip, gate, dgated, span=SPAN):
    rows, chan = u.shape
    n = alog.shape[0]
    rank = lr.shape[1]
    steps = rows // span
    full = lambda a: pl.BlockSpec(a.shape, lambda i: (0,) * a.ndim)
    tok = lambda w: pl.BlockSpec((span, w), lambda i: (i, 0))
    return pl.pallas_call(
        fwd_kernel, grid=(steps,),
        in_specs=[tok(rank), full(dtw), full(dtb), tok(2*n), pl.BlockSpec((2*n, span), lambda i: (0, i)), tok(chan), full(alog), full(skip), tok(chan), tok(chan)],
        out_specs=[tok(chan)] * 3 + [pl.BlockSpec((1, n, chan), lambda i: (i, 0, 0))],
        out_shape=[jax.ShapeDtypeStruct((rows, chan), jnp.bfloat16)] * 3 + [jax.ShapeDtypeStruct((steps, n, chan), jnp.float32)],
        scratch_shapes=[pltpu.VMEM((n, chan), jnp.float32)] + [pltpu.VMEM((span, chan), jnp.float32)] * 3 + [pltpu.VMEM((span, TILE * n), jnp.bfloat16), pltpu.VMEM((span * n, chan), jnp.bfloat16)],
        compiler_params=pltpu.CompilerParams(vmem_limit_bytes=56 << 20),
    )(lr, dtw, dtb, cf, ct, u, alog, skip, gate, dgated)

def bwd_kernel(lr, dtw, dtb, cf, ct, u, alog, skip, dy, starts, dpre, dval, dlow, din, dout, galog, gskip, gbias, gdtw, lam_s, dt_s, du_s, dyf_s, hp_s, st_s, th_s, bd_s, hb_s, gb_s):
    span, chan = u.shape
    n = alog.shape[0]
    @pl.when(pl.program_id(0) == 0)
    def _():
        lam_s[...] = jnp.zeros_like(lam_s)
        galog[...] = jnp.zeros_like(galog)
        gskip[...] = jnp.zeros_like(gskip)
        gbias[...] = jnp.zeros_like(gbias)
        gdtw[...] = jnp.zeros_like(gdtw)
    decay = -jnp.exp(alog[...])
    rate = decay * LOG2E
    pre = mm(lr[...], dtw[...]) + dtb[...]
    dt = softplus(pre)
    uf = u[...].astype(jnp.float32)
    dyf = dy[...].astype(jnp.float32)
    dt_s[...] = dt
    du_s[...] = dt * uf
    dyf_s[...] = dyf
    bd_s[...] = spread(cf[:, :n], n)
    mask = diagonal(TILE, n)
    ones = mask.astype(jnp.bfloat16)
    block = FU * TILE
    def reduce_h(g):
        for k in range(FU):
            t0 = pl.multiple_of(g * block + k * TILE, TILE)
            cross = mt(dy[pl.ds(t0, TILE), :], hb_s[pl.ds(pl.multiple_of(t0 * n, TILE * n), TILE * n), :])
            dout[0, pl.ds(g * FU + k, 1), :] = jnp.sum(jnp.where(mask, cross, 0.0), axis=0, keepdims=True)
    def again(g, h):
        c = pltpu.roll(ct[:n, :], span - g * block, 1)
        reduce_h(jnp.maximum(g - 1, 0))
        for j in range(block):
            t = g * block + j
            hp_s[t] = h
            e = jnp.exp2(dt_s[pl.ds(t, 1), :] * rate)
            h = e * h + du_s[pl.ds(t, 1), :] * c[:, j:j+1]
            hb_s[pl.ds(pl.multiple_of(t * n, n), n), :] = h.astype(jnp.bfloat16)
        return h
    lax.fori_loop(0, span // block, again, starts[0])
    reduce_h(span // block - 1)
    back = BU * TILE
    per = span // back
    def reduce_lam(g):
        for k in range(BU - 1, -1, -1):
            t0 = pl.multiple_of(g * back + k * TILE, TILE)
            wide = pl.ds(pl.multiple_of(t0 * n, TILE * n), TILE * n)
            lam16 = hb_s[wide, :]
            st_s[pl.ds(t0, TILE), :] = mm(ones, gb_s[wide, :])
            th_s[pl.ds(t0, TILE), :] = mm(bd_s[pl.ds(t0, TILE), :], lam16)
            cross = mt(du_s[pl.ds(t0, TILE), :].astype(jnp.bfloat16), lam16)
            din[0, pl.ds(g * BU + k, 1), :] = jnp.sum(jnp.where(mask, cross, 0.0), axis=0, keepdims=True)
    def group(q, state):
        carry, gdec = state
        g = per - 1 - q
        c = pltpu.roll(ct[n:, :], span - g * back, 1)
        reduce_lam(jnp.minimum(g + 1, per - 1))
        for j in range(back - 1, -1, -1):
            t = g * back + j
            here = pl.ds(pl.multiple_of(t * n, n), n)
            d = dt_s[pl.ds(t, 1), :]
            lam = carry + dyf_s[pl.ds(t, 1), :] * c[:, j:j+1]
            carry = lam * jnp.exp2(d * rate)
            grow = carry * hp_s[t]
            gdec = gdec + grow * d
            hb_s[here, :] = lam.astype(jnp.bfloat16)
            gb_s[here, :] = (grow * decay).astype(jnp.bfloat16)
        return carry, gdec
    carry, gdec = lax.fori_loop(0, per, group, (lam_s[...], jnp.zeros_like(decay)))
    reduce_lam(0)
    lam_s[...] = carry
    galog[...] += gdec * decay
    gskip[...] += jnp.sum(dyf * uf, axis=0, keepdims=True)
    thru = th_s[...]
    dp = ((st_s[...] + thru * uf) * jax.nn.sigmoid(pre)).astype(jnp.bfloat16)
    dpre[...] = dp
    dval[...] = thru * dt + skip[...] * dyf
    gbias[...] += jnp.sum(dp.astype(jnp.float32), axis=0, keepdims=True)
    dlow[...] = mt(dp, dtw[...])
    gdtw[...] += lax.dot_general(lr[...], dp, (((0,), (0,)), ((), ())), preferred_element_type=jnp.float32)

def scan_backward(lr, dtw, dtb, cf, ct, u, alog, skip, dy, starts, span=SPAN):
    rows, chan = u.shape
    n = alog.shape[0]
    rank = lr.shape[1]
    steps = rows // span
    full = lambda a: pl.BlockSpec(a.shape, lambda i: (0,) * a.ndim)
    tok = lambda w: pl.BlockSpec((span, w), lambda i: (steps - 1 - i, 0))
    ctok = pl.BlockSpec((2*n, span), lambda i: (0, steps - 1 - i))
    ptok = pl.BlockSpec((1, span // TILE, TILE * n), lambda i: (steps - 1 - i, 0, 0))
    f = lambda *s: jax.ShapeDtypeStruct(s, jnp.float32)
    outs = [jax.ShapeDtypeStruct((rows, chan), jnp.bfloat16), f(rows, chan), f(rows, rank), f(steps, span // TILE, TILE * n), f(steps, span // TILE, TILE * n), f(n, chan), f(1, chan), f(1, chan), f(rank, chan)]
    return pl.pallas_call(
        bwd_kernel, grid=(steps,),
        in_specs=[tok(rank), full(dtw), full(dtb), tok(2*n), ctok, tok(chan), full(alog), full(skip), tok(chan), pl.BlockSpec((1, n, chan), lambda i: (steps - 1 - i, 0, 0))],
        out_specs=[tok(chan), tok(chan), tok(rank), ptok, ptok] + [full(o) for o in outs[5:]],
        out_shape=outs,
        scratch_shapes=[pltpu.VMEM((n, chan), jnp.float32)] + [pltpu.VMEM((span, chan), jnp.float32)] * 3 + [pltpu.VMEM((span, n, chan), jnp.float32)] + [pltpu.VMEM((span, chan), jnp.float32)] * 2 + [pltpu.VMEM((span, TILE * n), jnp.bfloat16)] + [pltpu.VMEM((span * n, chan), jnp.bfloat16)] * 2,
        compiler_params=pltpu.CompilerParams(vmem_limit_bytes=56 << 20),
    )(lr, dtw, dtb, cf, ct, u, alog, skip, dy, starts)


def shifted(block, before, back):
    if back == 0:
        return block
    rows = block.shape[0]
    return jnp.concatenate([before[8 - back :], block[: rows - back]], 0)


def masked_sum(x, masks, weights, product):
    total = None
    for m in range(weights[0].shape[0]):
        held = x * masks[:, m : m + 1]
        parts = [product(held, w[m]) for w in weights]
        total = parts if total is None else [t + p for t, p in zip(total, parts)]
    return total


def enter_kernel(rows, masks, w, cw, cb, xp, conv_in, gate_in, pre_act, conv_out, part, tail):
    @pl.when(pl.program_id(0) == 0)
    def _():
        tail[...] = jnp.zeros_like(tail)

    taps = cw.shape[0]
    unit = masks.shape[0] // rows.shape[0]
    x = jnp.concatenate([rows[k, :unit] for k in range(rows.shape[0])], 0)
    ax, az = masked_sum(x, masks[...], (w.at[0], w.at[1]), mm)
    before = tail[...]
    pre = cb[...]
    for k in range(taps):
        pre = pre + cw[k : k + 1] * shifted(ax, before, taps - 1 - k)
    tail[...] = ax[-8:]
    out = (pre * jax.nn.sigmoid(pre)).astype(jnp.bfloat16)
    conv_in[...] = ax
    gate_in[...] = az
    pre_act[...] = pre
    conv_out[...] = out
    part[...] = mm(out, xp[...])


def whole_spec(a):
    return pl.BlockSpec(a.shape, lambda i: (0,) * len(a.shape))


def enter(rows, masks, w, cw, cb, xp, block):
    wide, padded, width = rows.shape
    span = masks.shape[0]
    chan, small = xp.shape
    tok = lambda w: pl.BlockSpec((block, w), lambda i: (i, 0))
    f = lambda w, t=jnp.float32: jax.ShapeDtypeStruct((span, w), t)
    return pl.pallas_call(
        enter_kernel,
        grid=(span // block,),
        in_specs=[pl.BlockSpec((block * wide // span, padded, width), lambda i: (i, 0, 0)), tok(masks.shape[1])]
        + [whole_spec(a) for a in (w, cw, cb, xp)],
        out_specs=[tok(chan)] * 4 + [tok(small)],
        out_shape=[f(chan), f(chan), f(chan), f(chan, jnp.bfloat16), f(small)],
        scratch_shapes=[pltpu.VMEM((8, chan), jnp.float32)],
        compiler_params=pltpu.CompilerParams(vmem_limit_bytes=56 << 20),
    )(rows, masks, w, cw, cb, xp)


def apply_kernel(masks, *refs, turned):
    *inputs, w, out = refs
    total = None
    for k, x in enumerate(inputs):
        (part,) = masked_sum(x[...], masks[...], (w.at[k],), mt if turned else mm)
        total = part if total is None else total + part
    out[...] = total.astype(out.dtype)


def apply(masks, inputs, w, turned, dtype, block):
    span = masks.shape[0]
    width = w.shape[2 if turned else 3]
    tok = lambda c: pl.BlockSpec((block, c), lambda i: (i, 0))
    return pl.pallas_call(
        functools.partial(apply_kernel, turned=turned),
        grid=(span // block,),
        in_specs=[tok(masks.shape[1])] + [tok(x.shape[1]) for x in inputs] + [whole_spec(w)],
        out_specs=tok(width),
        out_shape=jax.ShapeDtypeStruct((span, width), dtype),
        compiler_params=pltpu.CompilerParams(vmem_limit_bytes=56 << 20),
    )(masks, *inputs, w)


def leave_kernel(dval, dsmall, xp, pre_act, conv_in, prev_in, conv_out, cw, d_conv_in, grad_taps, grad_bias, grad_x, head):
    i = pl.program_id(0)
    steps = pl.num_programs(0)

    @pl.when(i == 0)
    def _():
        head[...] = jnp.zeros_like(head)
        grad_taps[...] = jnp.zeros_like(grad_taps)
        grad_bias[...] = jnp.zeros_like(grad_bias)
        grad_x[...] = jnp.zeros_like(grad_x)

    taps = cw.shape[0]
    d_out = (dval[...] + mt(dsmall[...], xp[...])).astype(jnp.bfloat16).astype(jnp.float32)
    pre = pre_act[...]
    sig = jax.nn.sigmoid(pre)
    d_pre = d_out * sig * (1.0 + pre * (1.0 - sig))
    before = jnp.where(i == steps - 1, 0.0, prev_in[...])
    held = conv_in[...]
    rows = held.shape[0]
    after = head[...]
    total = None
    for k in range(taps):
        back = taps - 1 - k
        grad_taps[k : k + 1] += jnp.sum(d_pre * shifted(held, before, back), axis=0, keepdims=True)
        moved = d_pre if back == 0 else jnp.concatenate([d_pre[back:], after[:back]], 0)
        term = cw[k : k + 1] * moved
        total = term if total is None else total + term
    head[...] = d_pre[:8]
    d_conv_in[...] = total.astype(jnp.bfloat16)
    grad_bias[...] += jnp.sum(d_pre, axis=0, keepdims=True)
    grad_x[...] += lax.dot_general(conv_out[...], dsmall[...], (((0,), (0,)), ((), ())), preferred_element_type=jnp.float32)


def leave(dval, dsmall, xp, pre_act, conv_in, conv_out, cw, block):
    span, chan = pre_act.shape
    steps = span // block
    taps, small = cw.shape[0], xp.shape[1]
    tok = lambda w: pl.BlockSpec((block, w), lambda i: (steps - 1 - i, 0))
    prev = pl.BlockSpec((8, chan), lambda i: (jnp.maximum((steps - 1 - i) * (block // 8) - 1, 0), 0))
    f = lambda *s: jax.ShapeDtypeStruct(s, jnp.float32)
    outs = [jax.ShapeDtypeStruct((span, chan), jnp.bfloat16), f(taps, chan), f(1, chan), f(chan, small)]
    return pl.pallas_call(
        leave_kernel,
        grid=(steps,),
        in_specs=[tok(chan), tok(small), whole_spec(xp), tok(chan), tok(chan), prev, tok(chan), whole_spec(cw)],
        out_specs=[tok(chan)] + [whole_spec(o) for o in outs[1:]],
        out_shape=outs,
        scratch_shapes=[pltpu.VMEM((8, chan), jnp.float32)],
        compiler_params=pltpu.CompilerParams(vmem_limit_bytes=56 << 20),
    )(dval, dsmall, xp, pre_act, conv_in, conv_in, conv_out, cw)


def sort_kernel(start, rank, *refs, pieces):
    inputs, out = refs[:-1], refs[-1]
    rows = out.shape[0]
    span = rank.shape[1]
    first = start[0] + pl.program_id(0) * rows
    here = lax.broadcasted_iota(jnp.int32, (rows, span), 0) + first
    choose = jnp.where(rank[...] == here, 1.0, 0.0).astype(jnp.bfloat16)
    at = 0
    for k in range(0, len(inputs), pieces):
        group = inputs[k : k + pieces]
        x = group[0][...] if pieces == 1 else jnp.concatenate([g[: span // pieces] for g in group], 0)
        out[:, at : at + x.shape[1]] = mm(choose, x).astype(out.dtype)
        at += x.shape[1]


def sort_rows(start, rank, inputs, rows, block, pieces=1):
    span = rank.shape[1]
    width = sum(x.shape[1] for x in inputs) // pieces
    return pl.pallas_call(
        functools.partial(sort_kernel, pieces=pieces),
        grid_spec=pltpu.PrefetchScalarGridSpec(
            num_scalar_prefetch=1,
            grid=(rows // block,),
            in_specs=[pl.BlockSpec((1, span), lambda i, s: (0, 0))]
            + [pl.BlockSpec(x.shape, lambda i, s: (0, 0)) for x in inputs],
            out_specs=pl.BlockSpec((block, width), lambda i, s: (i, 0)),
        ),
        out_shape=jax.ShapeDtypeStruct((rows, width), inputs[0].dtype),
        compiler_params=pltpu.CompilerParams(vmem_limit_bytes=56 << 20),
    )(start, rank, *inputs)


def blocks_kernel(place, masks, *refs, pairs):
    blocks, w, out = refs[:-2], refs[-2], refs[-1]
    unit = blocks[0].shape[0]
    core, chip = place[0] % 2, place[0] // 2
    for k in range(pairs):
        here = pl.multiple_of((chip ^ k) * 2 * unit, 2 * unit)
        low = pl.ds(pl.multiple_of(here + core * unit, unit), unit)
        high = pl.ds(pl.multiple_of(here + (1 - core) * unit, unit), unit)
        x = jnp.concatenate([blocks[2 * k][...], blocks[2 * k + 1][...]], 0)
        marks = jnp.concatenate([masks[low, :], masks[high, :]], 0)
        (total,) = masked_sum(x, marks, (w,), mt)
        out[low, :] = total[:unit]
        out[high, :] = total[unit:]


def apply_blocks(place, masks, blocks, w):
    span, chan = masks.shape[0], w.shape[1]
    return pl.pallas_call(
        functools.partial(blocks_kernel, pairs=len(blocks) // 2),
        grid_spec=pltpu.PrefetchScalarGridSpec(
            num_scalar_prefetch=1,
            grid=(1,),
            in_specs=[pl.BlockSpec(a.shape, lambda i, s, n=a.ndim: (0,) * n) for a in (masks, *blocks, w)],
            out_specs=pl.BlockSpec((span, chan), lambda i, s: (0, 0)),
        ),
        out_shape=jax.ShapeDtypeStruct((span, chan), jnp.float32),
        compiler_params=pltpu.CompilerParams(vmem_limit_bytes=56 << 20),
    )(place, masks, *blocks, w)


def contract(left, right, left_dim, right_dim):
    return lax.dot_general(
        left, right, (((left_dim,), (right_dim,)), ((), ())), preferred_element_type=jnp.float32
    )


def own(array, dim, size):
    return lax.dynamic_slice_in_dim(array, lax.axis_index("wide") * size, size, dim)


def pick(array, index, dim=0):
    return lax.dynamic_index_in_dim(array, index, dim, False)


def cross(array, k):
    return lax.ppermute(array, "wide", [(i, i ^ k) for i in range(lax.axis_size("wide"))])


def begin_gather(shard):
    if lax.axis_size("wide") != 8:
        return (shard,)
    return shard, cross(shard, 2), cross(shard, 4), cross(shard, 1)


def end_gather(begun, work):
    if lax.axis_size("wide") != 8:
        whole = lax.all_gather(begun[0], "wide", axis=0)
        return [whole[k] for k in range(whole.shape[0])], work()
    shard, by_x, by_y, pair = begun
    half = shard.shape[0] // 2
    far = (cross(by_y[:half], 2), cross(by_x[half:], 4))
    pair_x, pair_y = cross(by_x, 1), cross(by_y, 1)
    beside, *far = lax.optimization_barrier((work(),) + far)
    far = jnp.concatenate(far, 0)
    return [shard, pair, by_x, pair_x, by_y, pair_y, far, cross(far, 1)], beside


def assemble(blocks):
    if lax.axis_size("wide") != 8:
        return jnp.stack(blocks)
    here = lax.axis_index("wide")
    whole = jnp.zeros((8,) + blocks[0].shape, blocks[0].dtype)
    for k, block in enumerate(blocks):
        whole = lax.dynamic_update_index_in_dim(whole, block, here ^ k, 0)
    return whole


def sum_wide(part, held, work, ordered=True):
    if lax.axis_size("wide") != 8:
        return lax.psum(part, "wide"), work(held)
    half = part.shape[0] // 2
    core = lax.axis_index("wide") % 2
    mine = lax.dynamic_slice_in_dim(part, core * half, half, 0)
    other = lax.dynamic_slice_in_dim(part, (1 - core) * half, half, 0)
    mine = mine + cross(other, 1)
    if ordered:
        mine, held = lax.optimization_barrier((mine, held))
    sent = mine.astype(jnp.bfloat16)
    beside, *came = lax.optimization_barrier((work(held),) + tuple(cross(sent, k) for k in (2, 4, 6)))
    total = mine
    for block in came:
        total = total + block.astype(jnp.float32)
    other = cross(total, 1)
    return jnp.where(core == 0, jnp.concatenate([total, other], 0), jnp.concatenate([other, total], 0)), beside


def scatter_wide(part):
    return lax.psum_scatter(part, "wide", scatter_dimension=0, tiled=True).astype(jnp.float32)


def after(value, *first):
    return lax.optimization_barrier((value,) + first)[0]


def hop(rising, falling):
    return (
        lax.ppermute(rising, "row", [(0, 1), (1, 2), (2, 3)]),
        lax.ppermute(falling, "row", [(1, 0), (2, 1), (3, 2)]),
    )


def near_slot(hops, side):
    here = lax.axis_index("row")
    return (hops[0][0], hops[0][1]), jnp.where(here == 0, 1, 0), side


def middle_slot(hops, side):
    return (hops[1][0], hops[1][1]), jnp.where(lax.axis_index("row") < 2, 1, 0), side


def last_slot(hops, side):
    here = lax.axis_index("row")
    return (hops[0][1], hops[2][0], hops[2][1]), jnp.where(here == 3, 1, jnp.where(here == 0, 2, 0)), side


def only(array, side):
    return (array,), 0, side


def sum_row(part):
    if lax.axis_size("row") != 4:
        return lax.psum(part, "row")
    for k in (1, 2):
        part = part + lax.ppermute(part, "row", [(i, i ^ k) for i in range(4)])
    return part


def sum_row_low(part, beside):
    if lax.axis_size("row") != 4:
        return lax.psum(part.astype(jnp.bfloat16), "row").astype(jnp.float32), beside
    for k in (1, 2):
        sent = lax.ppermute(part.astype(jnp.bfloat16), "row", [(i, i ^ k) for i in range(4)])
        if k == 1:
            sent, beside = lax.optimization_barrier((sent, beside))
        part = part + sent.astype(jnp.float32)
    return part, beside


def share_wide(part):
    count = lax.axis_size("wide")
    if count != 8:
        return lax.psum_scatter(part, "wide", scatter_dimension=0, tiled=True)
    for k in (1, 2, 4):
        part = part + cross(part, k)
    return own(part, 0, part.shape[0] // count)


def row_order():
    count = lax.axis_size("row")
    here = lax.axis_index("row")
    if count != 4:
        return [lax.rem(here + s, count) for s in range(count)]
    near = jnp.where(here == 0, 1, here - 1)
    last = jnp.where(here == 3, 0, jnp.where(here == 0, 3, here + 1))
    return [here, near, lax.rem(here + 2, 4), last]


def others(array, order):
    return jnp.stack([pick(array, q) for q in order[1:]], 0)


def gather_ordered(block, order):
    whole = lax.all_gather(block, "row", axis=0)
    return [block] + [pick(whole, q) for q in order[1:]]


def sorted_places(ids, mods):
    one = (ids[:, None] == jnp.arange(mods, dtype=ids.dtype)[None]).astype(jnp.int32)
    before = jnp.cumsum(one, 0)
    total = before[-1]
    first = jnp.cumsum(total) - total
    return jnp.sum(one * (before - 1 + first[None]), 1)[None]


def group_bounds(ids, mods):
    count = jnp.sum((ids[:, None] == jnp.arange(mods, dtype=ids.dtype)).astype(jnp.int32), 0)
    return jnp.concatenate([jnp.zeros((1,), jnp.int32), jnp.cumsum(count)], 0)


def local(
    hidden,
    modality,
    norm_gain,
    in_proj,
    conv_weight,
    conv_bias,
    x_proj_dt,
    x_proj_bc,
    dt_proj,
    dt_bias,
    a_log,
    skip_weight,
    out_proj,
    cotangent,
):
    shard_rows, width = hidden.shape
    mods = in_proj.shape[0]
    chan = in_proj.shape[3]
    taps = conv_weight.shape[0]
    n = a_log.shape[0]
    rank = dt_proj.shape[0]
    row_count = lax.axis_size("row")
    residual = hidden.astype(jnp.float32)
    inv_rms = lax.rsqrt(jnp.mean(residual * residual, axis=-1, keepdims=True) + EPS)
    gain_vec = norm_gain.astype(jnp.float32)
    normed = (residual * inv_rms * gain_vec).astype(jnp.bfloat16)
    lanes = jnp.pad(modality.astype(jnp.bfloat16)[None], ((0, 15), (0, width - shard_rows)))
    conv_taps = conv_weight.astype(jnp.float32)
    w_out = out_proj[None]

    def small_slices():
        x_proj = jnp.concatenate([own(x_proj_dt, 0, chan), own(x_proj_bc, 0, chan)], 1)
        return x_proj, own(dt_proj, 1, chan), own(dt_bias, 0, chan)[None], own(a_log, 1, chan), own(skip_weight, 0, chan)[None]

    begun = begin_gather(jnp.concatenate([normed, lanes], 0))
    begun, w_in = lax.optimization_barrier((begun, jnp.transpose(in_proj, (2, 0, 1, 3))))
    row_blocks, (x_proj, dtw, dtb, alog, skip) = end_gather(begun, small_slices)
    rows = assemble(row_blocks)
    ids = rows[:, shard_rows, :shard_rows].astype(jnp.int32).reshape(-1)
    masks = (ids[:, None] == jnp.arange(128, dtype=ids.dtype)[None]).astype(jnp.bfloat16)
    span_rows = ids.shape[0]
    block = min(256, span_rows)
    order = row_order()
    slot = jnp.arange(row_count, dtype=jnp.int32)[:, None] == lax.axis_index("row")
    whole = jnp.zeros((1,), jnp.int32)
    chunk = lax.axis_index("wide").astype(jnp.int32)[None] * shard_rows
    places = sorted_places(ids, mods)
    pieces = len(row_blocks)
    here = lax.axis_index("wide").astype(jnp.int32)
    if pieces == 8:
        swapped = places.reshape(pieces, shard_rows)
        block_places = jnp.concatenate([pick(swapped, here ^ k)[None] for k in range(pieces)], 1)
    else:
        block_places = places
    rows_chunk = sort_rows(chunk, block_places, row_blocks, shard_rows, shard_rows, pieces)
    rows, rows_chunk = lax.optimization_barrier((rows, rows_chunk))
    rows_near = lax.all_gather(rows_chunk, "row", axis=0)
    cot_begun = begin_gather(after(cotangent, rows_chunk))
    conv_in, gate_in, pre_act, conv_out, part = enter(
        rows, masks, w_in, conv_taps, conv_bias.astype(jnp.float32)[None], x_proj, block
    )
    part, cot_begun = lax.optimization_barrier((part, cot_begun))

    cot_blocks, _ = end_gather(cot_begun, lambda: ())

    def first_work(cot_blocks):
        cot_chunk = sort_rows(chunk, block_places, cot_blocks, shard_rows, shard_rows, pieces)
        if pieces == 8:
            d_gated = apply_blocks(here[None], masks, cot_blocks, out_proj)
        else:
            d_gated = apply(masks, (jnp.concatenate(cot_blocks, 0),), w_out, True, jnp.float32, block)
        return cot_chunk, d_gated

    small, (cot_chunk, d_gated) = sum_wide(part, cot_blocks, first_work, False)
    cot_near = lax.all_gather(cot_chunk, "row", axis=0)
    low_rank = small[:, :rank].astype(jnp.bfloat16)
    coefs = small[:, rank:]
    gated, d_y, d_gate_in, starts = scan_forward(
        low_rank, dtw, dtb, coefs, coefs.T, conv_out, alog, skip, gate_in, d_gated
    )
    line = row_count == 4
    gates = sort_rows(whole, places, (gated, d_gate_in), span_rows, block)
    bounds = sum_row(jnp.where(slot, group_bounds(after(ids, part), mods)[None], 0))
    bounds = jnp.stack([pick(bounds, q) for q in order], 0)
    d_y, gates, bounds, rows_near = lax.optimization_barrier((d_y, gates, bounds, rows_near))
    rows_far = lax.all_gather(others(rows_near, order), "wide", axis=0)
    gate_hops = [hop(gates, gates)] if line else []
    d_pre_step, d_value, d_low_part, d_in, d_out, grad_alog, grad_skip, grad_bias, grad_wdtp = scan_backward(
        low_rank, dtw, dtb, coefs, coefs.T, conv_out, alog, skip, d_y, starts
    )
    d_part = jnp.concatenate([d_low_part, d_in.reshape(span_rows, n), d_out.reshape(span_rows, n)], 1)
    d_part, cot_near, gate_hops = lax.optimization_barrier((d_part, cot_near, gate_hops))
    cot_far = lax.all_gather(others(cot_near, order), "wide", axis=0)

    def third_work(gated):
        part = apply(masks, (gated,), w_out, False, jnp.bfloat16, block)
        return part

    d_small, projected = sum_wide(d_part, gated, third_work)
    if line:
        gate_hops.append(hop(*gate_hops[0]))
    d_small = d_small.astype(jnp.bfloat16)
    d_conv_in, grad_taps, grad_cbias, grad_x = leave(
        d_value, d_small, x_proj, pre_act, conv_in, conv_out, conv_taps, block
    )
    conv_sorted = sort_rows(whole, places, (d_conv_in,), span_rows, block)
    d_conv_in, conv_sorted = lax.optimization_barrier((d_conv_in, conv_sorted))
    conv_hops = [hop(conv_sorted, conv_sorted)] if line else []
    normed_part = apply(masks, (d_conv_in, d_gate_in), w_in, True, jnp.bfloat16, block)
    normed_part, rows_far = lax.optimization_barrier((normed_part, rows_far))
    if line:
        normed_part, gate_hops[1], conv_hops[0] = lax.optimization_barrier((normed_part, gate_hops[1], conv_hops[0]))
        gate_hops.append(hop(*gate_hops[1]))
        conv_hops.append(hop(*conv_hops[0]))
    rows_sorted = sort_rows(whole, block_places, [after(x, normed_part) for x in row_blocks], span_rows, block, pieces)
    cot_sorted = sort_rows(whole, block_places, [after(x, normed_part) for x in cot_blocks], span_rows, block, pieces)
    if line:
        rows_sorted, cot_sorted = lax.optimization_barrier((rows_sorted, cot_sorted))
        gates_all = lambda side: [only(gates, side), near_slot(gate_hops, side), middle_slot(gate_hops, side)]
    else:
        gates_rows = gather_ordered(gates, order)
        gates_all = lambda side: [only(g, side) for g in gates_rows]
        conv_all = [only(d, 0) for d in gather_ordered(conv_sorted, order)]
    apart = lambda a: a.reshape(span_rows // shard_rows, 1, shard_rows, width)
    far = range(row_count - 1)
    rows_slots = [(apart(rows_sorted), 0)] + [(rows_far, s) for s in far]
    cot_slots = [(apart(cot_sorted), 0)] + [(cot_far, s) for s in far]
    most = len(far)
    z_most = grad_in(bounds[:-1], rows_slots[:-1], [(g,) for g in gates_all(1)[:most]], mods, chan)
    d_normed = scatter_wide(normed_part)
    weighted = gain_vec * d_normed
    grad_hidden = (
        cotangent.astype(jnp.float32)
        + inv_rms * weighted
        - residual * inv_rms * inv_rms * inv_rms * jnp.mean(weighted * residual, axis=-1, keepdims=True)
    )
    g_gain = sum_row(share_wide(jnp.sum(d_normed * residual * inv_rms, 0)))

    small_grads = (grad_taps, grad_cbias[0], grad_x, grad_wdtp, grad_bias[0], grad_alog, grad_skip[0])
    flat = after(jnp.concatenate([g.reshape(-1) for g in small_grads]).reshape(-1, 128), z_most)
    z_most, cot_far = lax.optimization_barrier((z_most, cot_far))
    cot_slots = [(apart(cot_sorted), 0)] + [(cot_far, s) for s in far]
    if line:
        z_most, gate_hops[2], conv_hops[1] = lax.optimization_barrier((z_most, gate_hops[2], conv_hops[1]))
        conv_hops.append(hop(*conv_hops[1]))
        conv_all = [only(conv_sorted, 0), near_slot(conv_hops, 0), middle_slot(conv_hops, 0)]
        gates_all = [[*gates_all(side), last_slot(gate_hops, side)] for side in (0, 1)]
    else:
        gates_all = [gates_all(0), gates_all(1)]
    x_most = grad_in(bounds[:-1], rows_slots[:-1], [(d,) for d in conv_all[:most]], mods, chan)
    output = (residual + scatter_wide(after(projected, normed_part))).astype(jnp.bfloat16)
    flat, x_most = sum_row_low(flat, x_most)
    grad_wout = grad_out(bounds, cot_slots, gates_all[0], mods, chan)
    if line:
        x_most, grad_wout, conv_hops[2] = lax.optimization_barrier((x_most, grad_wout, conv_hops[2]))
        conv_all.append(last_slot(conv_hops, 0))
    grad_win = grad_in(bounds[-1:], rows_slots[-1:], [(conv_all[-1], gates_all[1][-1])], mods, chan, (x_most, z_most))
    grad_win = grad_win.reshape(mods, width, chan // 128, 2, 128).transpose(0, 1, 3, 2, 4).reshape(mods, width, 2, chan)
    flat = flat.reshape(-1)
    summed, at = [], 0
    for g in small_grads:
        summed.append(flat[at : at + g.size].reshape(g.shape))
        at += g.size
    g_taps, g_cbias, g_x, g_wdtp, g_bias, g_alog, g_skip = summed
    return (
        output,
        grad_hidden,
        g_gain,
        grad_win,
        g_taps,
        g_cbias,
        g_x[:, :rank],
        g_x[:, rank:],
        g_wdtp,
        g_bias,
        g_alog,
        g_skip,
        grad_wout,
    )


def solution(mesh):
    return jax.shard_map(
        local,
        mesh=mesh,
        in_specs=(
            P(("row", "wide"), None),
            P(("row", "wide")),
            P(),
            P(None, None, None, "wide"),
            P(None, "wide"),
            P("wide"),
            P(),
            P(),
            P(),
            P(),
            P(),
            P(),
            P(None, "wide", None),
            P(("row", "wide"), None),
        ),
        out_specs=(
            P(("row", "wide"), None),
            P(("row", "wide"), None),
            P("wide"),
            P(None, None, None, "wide"),
            P(None, "wide"),
            P("wide"),
            P("wide", None),
            P("wide", None),
            P(None, "wide"),
            P("wide"),
            P(None, "wide"),
            P("wide"),
            P(None, "wide", None),
        ),
        check_vma=False,
    )
```
